256 devices in a mesh: ctx: 32 (over z, y_hi, core), doc: 8 (over x, y_lo).
Axes of the slice: x: 4, y: 4 (y_hi: 2, y_lo: 2; y = y_hi * 2 + y_lo), z: 8, core: 2. Of those that a mesh axis runs over, the one named last changes fastest.
Arguments:
- activations: float32 [8, 8192, 1024], P('doc', 'ctx'), may hold values from -60 to 60
- queries: float32 [8, 8192, 512], P('doc', 'ctx'), may hold values from -8 to 8
- d_out: float32 [8, 8192, 512], P('doc', 'ctx'), may hold values from -6 to 6
- w_kv: float32 [1024, 1024], replicated, may hold values from -1 to 1
- partner: int32 [8, 32], P('doc', 'ctx'), may hold values from 0 to 31, as said below
- block_mask: int32 [8, 32, 4, 4], P('doc', 'ctx'), may hold values from 0 to 1, as said below
Outputs:
- attended: float32 [8, 8192, 512], P('doc', 'ctx')
- grad_w_kv: float32 [1024, 1024], P('ctx', 'doc')
The draws below stay inside these ranges and needn't reach their ends.
Inputs may be any that keep to these rules, and one draw needn't show every extreme that they name: partner[d, i] = i XOR s_d, where s_d of 1 to 31 is the same for all shards of document d, so shards are matched in pairs. `block_mask`: any 0/1 values; a shard's mask may be all zero or all one, and partners' masks are independent.
All inputs are finite; a program needn't handle non-finite values.
Results may differ from the reference program's by a relative error of at most 0.0003.
Values sent between devices are 32-bit elements; how exact they have to be, the bound alone decides.
A program may use at most 64 MiB of HBM per device.

```python
import math
import jax
import jax.numpy as jnp
from jax import lax

D = 1024
HEAD = 64
TOK_DEV = 256
KW = 512
NB = 4
SEQ = 8192
DOCS = 8
TOKENS = 65536
N_CTX = 32


def draw_w_kv(key, part):
    values = jax.random.normal(jax.random.fold_in(key, 22), (D, 2 * KW), jnp.float32)
    return jnp.clip(values, -3.0, 3.0) / math.sqrt(D)


def draw_activations(key, part):
    values = jnp.clip(jax.random.normal(jax.random.fold_in(key, 23), (DOCS, SEQ, D), jnp.float32), -4.0, 4.0)
    return jnp.clip(values, -60.0, 60.0)


def draw_queries(key, part):
    values = jnp.clip(jax.random.normal(jax.random.fold_in(key, 24), (DOCS, SEQ, KW), jnp.float32), -4.0, 4.0)
    return values


def draw_partner(key, part):
    offsets = jax.random.randint(jax.random.fold_in(key, 31), (DOCS, 1), 1, N_CTX)
    shards = jnp.arange(N_CTX, dtype=jnp.int32)[None, :]
    return jnp.bitwise_xor(shards, offsets.astype(jnp.int32)).astype(jnp.int32)


def draw_block_mask(key, part):
    levels = jax.random.randint(jax.random.fold_in(key, 32), (DOCS, N_CTX, 1, 1), 1, 9)
    ticks = jax.random.randint(jax.random.fold_in(key, 33), (DOCS, N_CTX, NB, NB), 0, 8)
    return (ticks < levels).astype(jnp.int32)


def block_scale(stream_key, extent, split, low, largest):
    level, own = 1.0, jax.random.fold_in(stream_key, 6)
    for position, shards_of in split:
        draws = jnp.exp(jax.random.uniform(jax.random.fold_in(own, position), (shards_of,), jnp.float32, low / len(split), largest / len(split)))
        level = level * jnp.repeat(draws, extent[position] // shards_of).reshape([-1 if axis == position else 1 for axis in range(len(extent))])
    return level


def normal_values(own_key, extent, deviation, bound, split=(), kind=jnp.bfloat16):
    array = jax.random.normal(own_key, extent, jnp.float32) * deviation
    if len(split) > 0:
        array = block_scale(own_key, extent, split, -0.22, 0.18) * array
    return jnp.clip(array, min=-bound, max=bound).astype(kind)


def setup_inputs(seed: int = 0) -> dict:
    key_of = jax.random.split(jax.random.key(seed), 7)
    return {
        "activations": draw_activations(jax.random.fold_in(key_of[6], 71), 0),
        "queries": draw_queries(jax.random.fold_in(key_of[6], 71), 0),
        "d_out": normal_values(key_of[2], (DOCS, SEQ, KW), 1.0, 6.0, ((0, 8), (1, 32)), jnp.float32),
        "w_kv": draw_w_kv(jax.random.fold_in(key_of[6], 71), 0),
        "partner": draw_partner(jax.random.fold_in(key_of[6], 71), 0),
        "block_mask": draw_block_mask(jax.random.fold_in(key_of[6], 71), 0),
    }


highest = lax.Precision.HIGHEST
masked_score = -1e+30

def visible_keys(mask_blocks, count):
    block = count // mask_blocks.shape[0]
    partner_part = jnp.repeat(jnp.repeat(mask_blocks, block, axis=0), block, axis=1) == 1
    return jnp.concatenate([jnp.ones((count, count), jnp.bool_), partner_part], axis=1)

def attend_shard(query_rows, key_rows, value_rows, visible, cotangent):
    factor = 1.0 / math.sqrt(query_rows.shape[2])
    scores = jnp.einsum('qhd,khd->hqk', query_rows, key_rows, precision=highest) * factor
    scores = jnp.where(visible[None], scores, masked_score)
    maximum = lax.optimization_barrier(jnp.max(scores, axis=2, keepdims=True))
    raised = jnp.exp(scores - maximum)
    totals = lax.optimization_barrier(jnp.sum(raised, axis=2, keepdims=True))
    weights = raised / totals
    attended = jnp.einsum('hqk,khd->qhd', weights, value_rows, precision=highest)
    grad_weights = jnp.einsum('qhd,khd->hqk', cotangent, value_rows, precision=highest)
    row_dot = jnp.transpose(lax.optimization_barrier(jnp.sum(cotangent * attended, axis=2)))[:, :, None]
    grad_scores = weights * (grad_weights - row_dot)
    grad_keys = jnp.einsum('hqk,qhd->khd', grad_scores, query_rows, precision=highest) * factor
    grad_values = jnp.einsum('hqk,qhd->khd', weights, cotangent, precision=highest)
    return (attended, grad_keys, grad_values)

def reference(activations, queries, d_out, w_kv, partner, block_mask):
    width = queries.shape[2]
    heads = width // HEAD

    def one_document(carry, inputs):
        doc_rows, doc_queries, doc_grads, doc_partner, doc_mask = inputs
        pairs = jnp.dot(doc_rows, w_kv, precision=highest)
        shards = pairs.reshape(N_CTX, TOK_DEV, 2 * width)

        def one_shard(shard):
            other = doc_partner[shard].astype(jnp.int32)
            own_pairs = lax.dynamic_index_in_dim(shards, shard, 0, keepdims=False)
            far_pairs = lax.dynamic_index_in_dim(shards, other, 0, keepdims=False)
            joined = jnp.concatenate([own_pairs, far_pairs], axis=0)
            key_rows = joined[:, :width].reshape(2 * TOK_DEV, heads, HEAD)
            value_rows = joined[:, width:].reshape(2 * TOK_DEV, heads, HEAD)
            start = (shard * TOK_DEV).astype(jnp.int32)
            query_rows = lax.dynamic_slice_in_dim(doc_queries, start, TOK_DEV, 0).reshape(TOK_DEV, heads, HEAD)
            cotangent = lax.dynamic_slice_in_dim(doc_grads, start, TOK_DEV, 0).reshape(TOK_DEV, heads, HEAD)
            visible = visible_keys(lax.dynamic_index_in_dim(doc_mask, shard, 0, keepdims=False), TOK_DEV)
            attended, grad_keys, grad_values = attend_shard(query_rows, key_rows, value_rows, visible, cotangent)
            grad_pairs = jnp.concatenate([grad_keys.reshape(2 * TOK_DEV, width), grad_values.reshape(2 * TOK_DEV, width)], axis=1)
            return (attended.reshape(TOK_DEV, width), grad_pairs)
        attended, grad_pairs = lax.map(one_shard, jnp.arange(N_CTX, dtype=jnp.int32))
        own_grads = grad_pairs[:, :TOK_DEV]
        far_grads = grad_pairs[:, TOK_DEV:]
        summed = own_grads + far_grads[doc_partner.astype(jnp.int32)]
        term = jnp.dot(jnp.transpose(doc_rows), summed.reshape(SEQ, 2 * width), precision=highest)
        return (carry + term, attended.reshape(SEQ, width))
    start_sum = jnp.zeros((D, 2 * KW), jnp.float32)
    grad_sum, attended = lax.scan(one_document, start_sum, (activations, queries, d_out, partner, block_mask))
    return (attended, grad_sum * (1.0 / math.sqrt(TOKENS)))
```

```python
import functools

import jax
import jax.numpy as jnp
from jax import lax
from jax.experimental import pallas as pl
from jax.experimental.pallas import tpu as pltpu
from jax.sharding import PartitionSpec as P

MESH = pl.DeviceIdType.MESH
F32, BF16 = jnp.float32, jnp.bfloat16
MASKED = -1e30
SLOTS = 16
CHUNKS = 8
MIB = 1024 * 1024


def split(x):
    hi = x.astype(BF16)
    return hi, (x - hi.astype(F32)).astype(BF16)


def nt_dot(a, b):
    return lax.dot_general(a, b, (((1,), (1,)), ((), ())), preferred_element_type=F32)


def nn_dot(a, b):
    return lax.dot_general(a, b, (((1,), (0,)), ((), ())), preferred_element_type=F32)


def remote(src, dst, send_sem, recv_sem, device):
    return pltpu.make_async_remote_copy(
        src_ref=src, dst_ref=dst, send_sem=send_sem, recv_sem=recv_sem,
        device_id=device, device_id_type=MESH,
    )


def exchange_kernel(partner_ref, act_ref, far_ref, core_in, base, y_in, z_out, z_in, dest,
                    core_s, core_r, y_s, y_r, z_s, z_r):
    me = lax.axis_index("ctx")
    z, rest = me // 4, me % 4
    core, yhi = me % 2, (me // 2) % 2
    core_dev = {"ctx": me + 1 - 2 * core}
    y_dev = {"ctx": me + 2 - 4 * yhi}
    right = {"ctx": ((z + 1) % 8) * 4 + rest}
    left = {"ctx": ((z + 7) % 8) * 4 + rest}
    z_dev = (right, left)
    barrier = pltpu.get_barrier_semaphore()
    for device in (core_dev, y_dev, right, left):
        pl.semaphore_signal(barrier, inc=1, device_id=device, device_id_type=MESH)
    pl.semaphore_wait(barrier, 4)

    offset = jnp.bitwise_xor(partner_ref[0, 0], me)
    flip_core = offset % 2 == 1
    flip_y = (offset // 2) % 2 == 1
    sz = offset // 4
    is4, is5 = sz == 4, sz == 5
    two = jnp.logical_or(sz == 2, sz == 6)
    three = jnp.logical_or(sz == 3, sz == 7)
    turned = sz >= 6
    is4_5 = jnp.logical_or(is4, is5)
    facing = (z, 7 - z)
    role = [jnp.where(turned, (zd + 2) % 4, zd % 4) for zd in facing]
    odd = [zd % 2 == 1 for zd in facing]

    rows = act_ref.shape[0] // CHUNKS
    order = (1, 0, 3, 2, 5, 4, 7, 6)
    core_cp, y_cp, z_cp = {}, {}, {}
    for j in order:
        core_cp[j] = remote(act_ref.at[pl.ds(j * rows, rows)], core_in.at[j], core_s.at[j], core_r.at[j], core_dev)
        core_cp[j].start()

    def own(j):
        if j % 2 == 1:
            return jnp.where(flip_y, y_in[j], base[j])
        return base[j]

    def ready(j):
        if j not in seen:
            seen.add(j)
            core_cp[j].wait_recv()
            base[j] = jnp.where(flip_core, core_in[j], act_ref[pl.ds(j * rows, rows)])
            if j % 2 == 1:
                y_cp[j] = remote(base.at[j], y_in.at[j], y_s.at[j], y_r.at[j], y_dev)
                y_cp[j].start()

    seen, arrived = set(), set()

    def want(j):
        ready(j)
        if j % 2 == 1 and j not in arrived:
            arrived.add(j)
            y_cp[j].wait_recv()

    for j in (1, 3, 5, 7, 0):
        ready(j)

    def got(t):
        for d in range(2):
            if (d, t) not in arrived:
                arrived.add((d, t))
                z_cp[d, t].wait_recv()

    for t in range(SLOTS):
        for d in range(2):
            if t < 4:
                want(t)
                want(2 * t + d)
                value = jnp.where(is4, own(2 * t + d), own(t))
            elif t < 8:
                got(t - 4)
                want(t)
                relay = jnp.logical_or(is4, jnp.logical_or(
                    jnp.logical_and(is5, jnp.logical_not(odd[d])), jnp.logical_and(three, role[d] == 1)))
                value = jnp.where(relay, z_in[d, t - 4], own(t))
            elif t < 12:
                got(t - 4)
                value = jnp.where(jnp.logical_or(is4_5, three), z_in[d, t - 4], z_in[d, t - 8])
            else:
                got(t - 4)
                late = jnp.logical_and(three, role[d] == 1)
                value = jnp.where(jnp.logical_or(is4_5, three), z_in[d, t - 4], z_in[d, t - 8])
                value = jnp.where(late, own(t - 8), value)
            z_out[d, t] = value
            z_cp[d, t] = remote(z_out.at[d, t], z_in.at[d, t], z_s.at[d, t], z_r.at[d, t], z_dev[d])
            z_cp[d, t].start()

    for k in range(CHUNKS):
        got(8 + k)
        got(12 + k // 2)
        value = own(k)
        for d in range(2):
            early = jnp.logical_and(sz == 1, odd[d])
            late = jnp.logical_or(
                jnp.logical_and(two, role[d] >= 2),
                jnp.logical_or(jnp.logical_and(three, role[d] == 3), jnp.logical_and(is5, jnp.logical_not(odd[d]))))
            near = jnp.logical_and(three, role[d] == 2)
            if k < 4:
                early = jnp.logical_or(early, near)
            else:
                late = jnp.logical_or(late, near)
            value = jnp.where(early, z_in[d, k], value)
            value = jnp.where(late, z_in[d, 8 + k], value)
        value = jnp.where(is4, z_in[k % 2, 12 + k // 2], value)
        if k % 2 == 0:
            dest[k] = value
            y_cp[k] = remote(dest.at[k], y_in.at[k], y_s.at[k], y_r.at[k], y_dev)
            y_cp[k].start()
        else:
            far_ref[pl.ds(k * rows, rows)] = value
    for k in range(0, CHUNKS, 2):
        y_cp[k].wait_recv()
        far_ref[pl.ds(k * rows, rows)] = jnp.where(flip_y, y_in[k], dest[k])
    for copies in (core_cp, y_cp, z_cp):
        for copy in copies.values():
            copy.wait_send()


def exchange(act, partner):
    count, depth = act.shape
    rows = count // CHUNKS
    chunk = lambda *lead: pltpu.VMEM(lead + (rows, depth), F32)
    dma = pltpu.SemaphoreType.DMA
    return pl.pallas_call(
        exchange_kernel,
        out_shape=jax.ShapeDtypeStruct((count, depth), F32),
        in_specs=[pl.BlockSpec(memory_space=pltpu.SMEM), pl.BlockSpec(memory_space=pltpu.VMEM)],
        out_specs=pl.BlockSpec(memory_space=pltpu.VMEM),
        scratch_shapes=[
            chunk(CHUNKS), chunk(CHUNKS), chunk(CHUNKS), chunk(2, SLOTS), chunk(2, SLOTS), chunk(CHUNKS),
            dma((CHUNKS,)), dma((CHUNKS,)), dma((CHUNKS,)), dma((CHUNKS,)), dma((2, SLOTS)), dma((2, SLOTS)),
        ],
        compiler_params=pltpu.CompilerParams(collective_id=0, has_side_effects=True, vmem_limit_bytes=32 * MIB),
    )(partner, act)


def attend(mask_ref, kv_hi, kv_lo, q_ref, d_ref, att_ref, g_hi, g_lo, s_ref, c_ref, w_hi, w_lo, t_hi, t_lo, pair):
    count, keys = q_ref.shape[0], kv_hi.shape[0]
    half = kv_hi.shape[1] // 2
    at = pl.ds(pl.multiple_of(pair * 128, 128), 128)
    at_v = pl.ds(pl.multiple_of(half + pair * 128, 128), 128)
    first = lax.broadcasted_iota(jnp.int32, (count, 128), 1) < 64
    k_h, k_l, v_h, v_l = kv_hi[:, at], kv_lo[:, at], kv_hi[:, at_v], kv_lo[:, at_v]

    def two_heads(x):
        return split(jnp.concatenate([jnp.where(first, x, 0.0), jnp.where(first, 0.0, x)], axis=0))

    q_h, q_l = two_heads(q_ref[:, at] * 0.125)
    d_h, d_l = two_heads(d_ref[:, at])
    cat = lambda *parts: jnp.concatenate(parts, axis=1)
    s_ref[...] = nt_dot(cat(k_h, k_h, k_l), cat(q_h, q_l, q_h))
    c_ref[...] = nt_dot(cat(v_h, v_h, v_l), cat(d_h, d_l, d_h))

    blocks, step = keys // 64, 64
    lanes = lax.broadcasted_iota(jnp.int32, (1, 2 * count), 1) % count // 64
    own_blocks = blocks // 2
    maximum = None
    for b in range(blocks):
        piece = s_ref[pl.ds(b * step, step), :]
        if b >= own_blocks:
            f = b - own_blocks
            seen = jnp.where(lanes == 0, mask_ref[0, f], jnp.where(lanes == 1, mask_ref[1, f], jnp.where(
                lanes == 2, mask_ref[2, f], mask_ref[3, f])))
            piece = jnp.where(seen == 1, piece, MASKED)
            s_ref[pl.ds(b * step, step), :] = piece
        top = jnp.max(piece, axis=0, keepdims=True)
        maximum = top if maximum is None else jnp.maximum(maximum, top)
    total, dots = 0.0, 0.0
    for b in range(blocks):
        rows = pl.ds(b * step, step)
        raised = jnp.exp(s_ref[rows, :] - maximum)
        s_ref[rows, :] = raised
        total = total + jnp.sum(raised, axis=0, keepdims=True)
        dots = dots + jnp.sum(raised * c_ref[rows, :], axis=0, keepdims=True)
    inverse = 1.0 / total
    row_dot = dots * inverse
    for b in range(blocks):
        rows = pl.ds(b * step, step)
        weight = s_ref[rows, :] * inverse
        w_hi[rows, :], w_lo[rows, :] = split(weight)
        t_hi[rows, :], t_lo[rows, :] = split(weight * (c_ref[rows, :] - row_dot))

    def grads(left_hi, left_lo, right_h, right_l):
        both = nn_dot(left_hi[...], cat(right_h, right_l))
        return both[:, :128] + both[:, 128:] + nn_dot(left_lo[...], right_h)

    g_hi[:, at], g_lo[:, at] = split(grads(t_hi, t_lo, q_h, q_l))
    g_hi[:, at_v], g_lo[:, at_v] = split(grads(w_hi, w_lo, d_h, d_l))
    flip = lambda x: x.astype(F32).T.astype(BF16)
    vt_h, vt_l = flip(v_h), flip(v_l)
    out = nn_dot(jnp.concatenate([vt_h, vt_l], axis=0), w_hi[...])
    out = out[:128] + out[128:] + nn_dot(vt_h, w_lo[...])
    att_ref[:, at] = jnp.concatenate([out[:64, :count], out[64:, count:]], axis=0).T


def main_kernel(mask_ref, own_ref, far_ref, q_ref, d_ref, w_ref, att_ref, grad_ref,
                a_hi, a_lo, at_hi, at_lo, kv_hi, kv_lo, g_hi, g_lo, s_ref, c_ref, w_hi, w_lo, t_hi, t_lo,
                term, core_in, total, ax_in, ax_sum, ay_in, by_in, by_sum, bx_in, z_out, z_in,
                core_s, core_r, ax_s, ax_r, ay_s, ay_r, by_s, by_r, bx_s, bx_r, z_s, z_r):
    ctx, doc = lax.axis_index("ctx"), lax.axis_index("doc")
    z, yhi, core = ctx // 4, (ctx // 2) % 2, ctx % 2
    x, ylo = doc // 2, doc % 2
    y = yhi * 2 + ylo

    def device(x_, y_, z_, core_):
        return {"ctx": z_ * 4 + (y_ // 2) * 2 + core_, "doc": x_ * 2 + y_ % 2}

    core_dev = device(x, y, z, 1 - core)
    x_dev = [None] + [device((x + n) % 4, y, z, core) for n in range(1, 4)]
    y_dev = [None] + [device(x, (y + n) % 4, z, core) for n in range(1, 4)]
    z_dev = [None] + [device(x, y, (z + n) % 8, core) for n in range(1, 8)]
    barrier = pltpu.get_barrier_semaphore()
    peers = [core_dev] + x_dev[1:] + y_dev[1:] + z_dev[1:]
    for peer in peers:
        pl.semaphore_signal(barrier, inc=1, device_id=peer, device_id_type=MESH)

    count = own_ref.shape[0]
    for n, ref in enumerate((own_ref, far_ref)):
        rows = pl.ds(n * count, count)
        a_hi[rows, :], a_lo[rows, :] = split(ref[...])
        at_hi[:, rows], at_lo[:, rows] = split(ref[...].T)

    def project(n, carry):
        at = pl.ds(pl.multiple_of(n * 256, 256), 256)
        p_h, p_l = split(w_ref[:, at])
        pairs = nn_dot(a_hi[...], p_h) + nn_dot(a_hi[...], p_l) + nn_dot(a_lo[...], p_h)
        kv_hi[:, at], kv_lo[:, at] = split(pairs)
        return carry

    lax.fori_loop(0, 4, project, 0)
    pl.semaphore_wait(barrier, len(peers))

    def pair_step(pair, carry):
        attend(mask_ref, kv_hi, kv_lo, q_ref, d_ref, att_ref, g_hi, g_lo, s_ref, c_ref, w_hi, w_lo, t_hi, t_lo, pair)
        return carry

    core_cp, ax_cp, ay_cp, by_cp, bx_cp, z_cp = {}, {}, {}, {}, {}, {}

    def term_step(block):
        at = pl.ds(block * 256, 256)
        value = nn_dot(at_hi[...], g_hi[:, at]) + nn_dot(at_hi[...], g_lo[:, at]) + nn_dot(at_lo[...], g_hi[:, at])
        value = value.reshape(8, 2, 2, 2, 16, 256)
        for c in range(2):
            for part in range(2):
                for yh in range(2):
                    for yl in range(2):
                        term[block, c, part, yh * 2 + yl] = value[:, yh, c, part, :, yl * 128:(yl + 1) * 128]
        core_cp[block] = remote(term.at[block, 1 - core], core_in.at[block], core_s.at[block], core_r.at[block], core_dev)
        core_cp[block].start()

    def sum_step(block):
        core_cp[block].wait_recv()
        total[block] = term[block, core] + core_in[block]

        @pl.when(block != x)
        def _():
            n = (block - x + 4) % 4
            remote(total.at[block, 0], ax_in.at[n - 1], ax_s.at[n - 1], ax_r.at[n - 1],
                   device(block, y, z, core)).start()

        for n in range(1, 4):
            by_cp[block, n] = remote(total.at[block, 1, (y + n) % 4], by_in.at[n - 1, block],
                                     by_s.at[n - 1, block], by_r.at[n - 1, block], y_dev[n])
            by_cp[block, n].start()

    lax.fori_loop(0, 2, pair_step, 0)
    term_step(0)
    term_step(2)
    lax.fori_loop(2, 4, pair_step, 0)
    sum_step(0)
    sum_step(2)
    term_step(1)
    term_step(3)
    sum_step(1)
    sum_step(3)

    value = total[x, 0]
    for n in range(1, 4):
        ax_cp[n] = remote(total.at[0, 0], ax_in.at[n - 1], ax_s.at[n - 1], ax_r.at[n - 1], x_dev[n])
        ax_cp[n].wait_recv()
        value = value + ax_in[n - 1]
    ax_sum[...] = value
    for n in range(1, 4):
        ay_cp[n] = remote(ax_sum.at[(y + n) % 4], ay_in.at[n - 1], ay_s.at[n - 1], ay_r.at[n - 1], y_dev[n])
        ay_cp[n].start()
    for block in range(4):
        value = total[block, 1, y]
        for n in range(1, 4):
            by_cp[block, n].wait_recv()
            value = value + by_in[n - 1, block]
        by_sum[block] = value
    for n in range(1, 4):
        bx_cp[n] = remote(by_sum.at[(x + n) % 4], bx_in.at[n - 1], bx_s.at[n - 1], bx_r.at[n - 1], x_dev[n])
        bx_cp[n].start()
    value = ax_sum[y]
    for n in range(1, 4):
        ay_cp[n].wait_recv()
        value = value + ay_in[n - 1]
    z_out[:, 0] = value
    value = by_sum[x]
    for n in range(1, 4):
        bx_cp[n].wait_recv()
        value = value + bx_in[n - 1]
    z_out[:, 1] = value
    for n in range(1, 8):
        z_cp[n] = remote(z_out.at[(z + n) % 8], z_in.at[n - 1], z_s.at[n - 1], z_r.at[n - 1], z_dev[n])
        z_cp[n].start()
    value = z_out[z]
    for n in range(1, 8):
        z_cp[n].wait_recv()
        value = value + z_in[n - 1]
    grad_ref[...] = value.reshape(32, 128) * (1.0 / 256.0)
    for copies in (core_cp, ax_cp, ay_cp, by_cp, bx_cp, z_cp):
        for copy in copies.values():
            copy.wait_send()


def attend_and_reduce(own, far, queries, cotangent, w_kv, mask):
    count, depth = own.shape
    vmem = pl.BlockSpec(memory_space=pltpu.VMEM)
    dma = pltpu.SemaphoreType.DMA
    f32 = lambda *shape: pltpu.VMEM(shape, F32)
    b16 = lambda *shape: pltpu.VMEM(shape, BF16)
    return pl.pallas_call(
        main_kernel,
        out_shape=(jax.ShapeDtypeStruct(queries.shape, F32), jax.ShapeDtypeStruct((32, 128), F32)),
        in_specs=[pl.BlockSpec(memory_space=pltpu.SMEM)] + [vmem] * 5,
        out_specs=(vmem, vmem),
        scratch_shapes=[
            b16(512, 1024), b16(512, 1024), b16(1024, 512), b16(1024, 512),
            b16(512, 1024), b16(512, 1024), b16(512, 1024), b16(512, 1024),
            f32(512, 512), f32(512, 512), b16(512, 512), b16(512, 512), b16(512, 512), b16(512, 512),
            f32(4, 2, 2, 4, 8, 16, 128), f32(4, 2, 4, 8, 16, 128), f32(4, 2, 4, 8, 16, 128),
            f32(3, 4, 8, 16, 128), f32(4, 8, 16, 128), f32(3, 8, 16, 128),
            f32(3, 4, 8, 16, 128), f32(4, 8, 16, 128), f32(3, 8, 16, 128),
            f32(8, 2, 16, 128), f32(7, 2, 16, 128),
            dma((4,)), dma((4,)), dma((3,)), dma((3,)), dma((3,)), dma((3,)),
            dma((3, 4)), dma((3, 4)), dma((3,)), dma((3,)), dma((7,)), dma((7,)),
        ],
        compiler_params=pltpu.CompilerParams(collective_id=1, has_side_effects=True, vmem_limit_bytes=56 * MIB),
    )(mask, own, far, queries, cotangent, w_kv)


def shards(activations, queries, d_out, w_kv, partner, block_mask):
    act = activations[0]
    far = exchange(act, partner)
    attended, gradient = attend_and_reduce(act, far, queries[0], d_out[0], w_kv, block_mask[0, 0])
    return attended[None], gradient


def solution(mesh):
    return jax.shard_map(
        shards,
        mesh=mesh,
        in_specs=(
            P("doc", "ctx", None), P("doc", "ctx", None), P("doc", "ctx", None),
            P(), P("doc", "ctx"), P("doc", "ctx", None, None),
        ),
        out_specs=(P("doc", "ctx", None), P("ctx", "doc")),
        check_vma=False,
    )
```

```python
import functools

import jax
import jax.numpy as jnp
from jax import lax
from jax.experimental import pallas as pl
from jax.experimental.pallas import tpu as pltpu
from jax.sharding import PartitionSpec as P

MESH = pl.DeviceIdType.MESH
F32, BF16 = jnp.float32, jnp.bfloat16
MASKED = -1e30
SLOTS = 16
CHUNKS = 8
MIB = 1024 * 1024


def split(x):
    hi = x.astype(BF16)
    return hi, (x - hi.astype(F32)).astype(BF16)


def nt_dot(a, b):
    return lax.dot_general(a, b, (((1,), (1,)), ((), ())), preferred_element_type=F32)


def nn_dot(a, b):
    return lax.dot_general(a, b, (((1,), (0,)), ((), ())), preferred_element_type=F32)


def remote(src, dst, send_sem, recv_sem, device):
    return pltpu.make_async_remote_copy(
        src_ref=src, dst_ref=dst, send_sem=send_sem, recv_sem=recv_sem,
        device_id=device, device_id_type=MESH,
    )


def head_pair(x, first):
    return split(jnp.concatenate([jnp.where(first, x, 0.0), jnp.where(first, 0.0, x)], axis=0))


def cat(*parts):
    return jnp.concatenate(parts, axis=1)


def scores(kv_hi, kv_lo, rows, at, right_h, right_l):
    hi, lo = kv_hi[rows, at], kv_lo[rows, at]
    return nt_dot(cat(hi, hi, lo), cat(right_h, right_l, right_h))


def lanes_of(pair, start=0):
    return pl.ds(pl.multiple_of(start + pair * 128, 128), 128)


BLOCK = 64


def own_part(pair, kv_hi, kv_lo, q_ref, d_ref, s_own, c_own, stats):
    count, half = q_ref.shape[0], kv_hi.shape[1] // 2
    first = lax.broadcasted_iota(jnp.int32, (count, 128), 1) < 64
    at, at_v = lanes_of(pair), lanes_of(pair, half)
    q_h, q_l = head_pair(q_ref[:, at] * 0.125, first)
    d_h, d_l = head_pair(d_ref[:, at], first)
    own = pl.ds(0, count)
    s_own[pair] = scores(kv_hi, kv_lo, own, at, q_h, q_l)
    c_own[pair] = scores(kv_hi, kv_lo, own, at_v, d_h, d_l)
    maximum = jnp.max(s_own[pair, pl.ds(0, BLOCK), :], axis=0, keepdims=True)
    for b in range(1, count // BLOCK):
        maximum = jnp.maximum(maximum, jnp.max(s_own[pair, pl.ds(b * BLOCK, BLOCK), :], axis=0, keepdims=True))
    total, dots = 0.0, 0.0
    for b in range(count // BLOCK):
        rows = pl.ds(b * BLOCK, BLOCK)
        raised = jnp.exp(s_own[pair, rows, :] - maximum)
        s_own[pair, rows, :] = raised
        total = total + jnp.sum(raised, axis=0, keepdims=True)
        dots = dots + jnp.sum(raised * c_own[pair, rows, :], axis=0, keepdims=True)
    stats[pair, pl.ds(0, 1), :] = maximum
    stats[pair, pl.ds(1, 1), :] = total
    stats[pair, pl.ds(2, 1), :] = dots


def far_part(pair, mask_ref, kv_hi, kv_lo, q_ref, d_ref, s_own, c_own, stats, s_far, c_far,
             w_hi, w_lo, t_hi, t_lo, att, g_hi, g_lo):
    count, half = q_ref.shape[0], kv_hi.shape[1] // 2
    first = lax.broadcasted_iota(jnp.int32, (count, 128), 1) < 64
    at, at_v = lanes_of(pair), lanes_of(pair, half)
    q_h, q_l = head_pair(q_ref[:, at] * 0.125, first)
    d_h, d_l = head_pair(d_ref[:, at], first)
    far = pl.ds(count, count)
    s_far[...] = scores(kv_hi, kv_lo, far, at, q_h, q_l)
    c_far[...] = scores(kv_hi, kv_lo, far, at_v, d_h, d_l)
    lanes = lax.broadcasted_iota(jnp.int32, (1, 2 * count), 1) % count // BLOCK
    own_max = stats[pair, pl.ds(0, 1), :]
    maximum = own_max
    blocks = count // BLOCK
    for b in range(blocks):
        rows = pl.ds(b * BLOCK, BLOCK)
        seen = jnp.where(lanes == 0, mask_ref[0, b], jnp.where(lanes == 1, mask_ref[1, b], jnp.where(
            lanes == 2, mask_ref[2, b], mask_ref[3, b])))
        piece = jnp.where(seen == 1, s_far[rows, :], MASKED)
        s_far[rows, :] = piece
        maximum = jnp.maximum(maximum, jnp.max(piece, axis=0, keepdims=True))
    shrink = jnp.exp(own_max - maximum)
    total = stats[pair, pl.ds(1, 1), :] * shrink
    dots = stats[pair, pl.ds(2, 1), :] * shrink
    for b in range(blocks):
        rows = pl.ds(b * BLOCK, BLOCK)
        raised = jnp.exp(s_far[rows, :] - maximum)
        s_far[rows, :] = raised
        total = total + jnp.sum(raised, axis=0, keepdims=True)
        dots = dots + jnp.sum(raised * c_far[rows, :], axis=0, keepdims=True)
    inverse = 1.0 / total
    row_dot = dots * inverse
    own_scale = shrink * inverse
    for b in range(blocks):
        rows = pl.ds(b * BLOCK, BLOCK)
        weight = s_own[pair, rows, :] * own_scale
        w_hi[rows, :], w_lo[rows, :] = split(weight)
        t_hi[rows, :], t_lo[rows, :] = split(weight * (c_own[pair, rows, :] - row_dot))
        lower = pl.ds(count + b * BLOCK, BLOCK)
        weight = s_far[rows, :] * inverse
        w_hi[lower, :], w_lo[lower, :] = split(weight)
        t_hi[lower, :], t_lo[lower, :] = split(weight * (c_far[rows, :] - row_dot))

    def grads(left_hi, left_lo, right_h, right_l):
        both = nn_dot(left_hi[...], cat(right_h, right_l))
        return both[:, :128] + both[:, 128:] + nn_dot(left_lo[...], right_h)

    g_hi[:, :128], g_lo[:, :128] = split(grads(t_hi, t_lo, q_h, q_l))
    g_hi[:, 128:], g_lo[:, 128:] = split(grads(w_hi, w_lo, d_h, d_l))
    flip = lambda value: value.astype(F32).T.astype(BF16)
    vt_h, vt_l = flip(kv_hi[:, at_v]), flip(kv_lo[:, at_v])
    out = nn_dot(jnp.concatenate([vt_h, vt_l], axis=0), w_hi[...])
    out = out[:128] + out[128:] + nn_dot(vt_h, w_lo[...])
    att[:, at] = jnp.concatenate([out[:64, :count], out[64:, count:]], axis=0).T


def kernel(partner_ref, mask_ref, act_hbm, q_hbm, d_hbm, w_hbm, att_hbm, grad_ref,
           act, far, q_ref, d_ref, w_ref, core_in, base, y_in, z_out, z_in, dest,
           p_hi, p_lo, a_hi, a_lo, at_hi, at_lo, kv_hi, kv_lo, g_hi, g_lo, s_own, c_own, stats, s_far, c_far,
           w_hi, w_lo, t_hi, t_lo, att,
           term, half_in, total, ax_in, ax_sum, ay_in, by_in, by_sum, bx_in, r_out, r_in,
           load_s, core_s, core_r, y_s, y_r, z_s, z_r,
           half_s, half_r, ax_s, ax_r, ay_s, ay_r, by_s, by_r, bx_s, bx_r, r_s, r_r):
    ctx, doc = lax.axis_index("ctx"), lax.axis_index("doc")
    z, yhi, core = ctx // 4, (ctx // 2) % 2, ctx % 2
    x, ylo = doc // 2, doc % 2
    y = yhi * 2 + ylo

    def device(x_, y_, z_, core_):
        return {"ctx": z_ * 4 + (y_ // 2) * 2 + core_, "doc": x_ * 2 + y_ % 2}

    core_dev = device(x, y, z, 1 - core)
    x_dev = [None] + [device((x + n) % 4, y, z, core) for n in range(1, 4)]
    y_dev = [None] + [device(x, (y + n) % 4, z, core) for n in range(1, 4)]
    z_dev = [None] + [device(x, y, (z + n) % 8, core) for n in range(1, 8)]
    far_y = y_dev[2]
    ring_dev = (z_dev[1], z_dev[7])
    barrier = pltpu.get_barrier_semaphore()
    peers = [core_dev] + x_dev[1:] + y_dev[1:] + z_dev[1:]
    for peer in peers:
        pl.semaphore_signal(barrier, inc=1, device_id=peer, device_id_type=MESH)
    loads = [pltpu.make_async_copy(src, dst, load_s.at[n]) for n, (src, dst) in enumerate(
        ((act_hbm, act), (w_hbm, w_ref), (q_hbm, q_ref), (d_hbm, d_ref)))]
    for load in loads:
        load.start()

    offset = jnp.bitwise_xor(partner_ref[0, 0], ctx)
    flip_core = offset % 2 == 1
    flip_y = (offset // 2) % 2 == 1
    sz = offset // 4
    both_ = jnp.logical_and
    either = jnp.logical_or
    is4, is5 = sz == 4, sz == 5
    two = either(sz == 2, sz == 6)
    three = either(sz == 3, sz == 7)
    steady = either(either(is4, is5), three)
    facing = (z, 7 - z)
    role = [jnp.where(sz >= 6, (zd + 2) % 4, zd % 4) for zd in facing]
    odd = [zd % 2 == 1 for zd in facing]
    count = act.shape[0]
    rows = count // CHUNKS
    core_cp, y_cp, z_cp, done = {}, {}, {}, set()

    def once(key, copy):
        if key not in done:
            done.add(key)
            copy.wait_recv()

    def chunk(ref, j):
        return ref[pl.ds(j * rows, rows), :]

    def send_core(j, src):
        core_cp[j] = remote(src, core_in.at[j], core_s.at[j], core_r.at[j], core_dev)
        core_cp[j].start()

    def send_y(j, src):
        y_cp[j] = remote(src, y_in.at[j], y_s.at[j], y_r.at[j], far_y)
        y_cp[j].start()

    def swap_core(j, value):
        once(("core", j), core_cp[j])
        return jnp.where(flip_core, core_in[j], value)

    def swap_y(j, value):
        once(("y", j), y_cp[j])
        return jnp.where(flip_y, y_in[j], value)

    def own(j):
        if j < 2:
            return chunk(act, j)
        return base[j] if j < 4 else swap_y(j, base[j])

    def got(t):
        for d in range(2):
            once((d, t), z_cp[d, t])

    def slot(t):
        for d in range(2):
            if t < 4:
                value = own(t) if d == t == 0 else jnp.where(is4, own(2 * t + d), own(t))
            elif t < 8:
                relay = either(is4, either(both_(is5, jnp.logical_not(odd[d])), both_(three, role[d] == 1)))
                value = jnp.where(relay, z_in[d, t - 4], own(t))
            else:
                value = jnp.where(steady, z_in[d, t - 4], z_in[d, t - 8])
                if t >= 12:
                    value = jnp.where(both_(three, role[d] == 1), own(t - 8), value)
            z_out[d, t] = value
            z_cp[d, t] = remote(z_out.at[d, t], z_in.at[d, t], z_s.at[d, t], z_r.at[d, t], ring_dev[d])
            z_cp[d, t].start()

    def arrived(k):
        value = own(k)
        for d in range(2):
            early = both_(sz == 1, odd[d])
            late = either(both_(two, role[d] >= 2),
                          either(both_(three, role[d] == 3), both_(is5, jnp.logical_not(odd[d]))))
            near = both_(three, role[d] == 2)
            if k < 4:
                early = either(early, near)
            else:
                late = either(late, near)
            value = jnp.where(early, z_in[d, k], value)
            value = jnp.where(late, z_in[d, 8 + k], value)
        return jnp.where(is4, z_in[k % 2, 12 + k // 2], value)

    def set_far(k, value):
        far[pl.ds(k * rows, rows), :] = value

    half = count // 2

    def take(ref, start, into, size):
        a_hi[pl.ds(into, size), :], a_lo[pl.ds(into, size), :] = split(ref[pl.ds(start, size), :])
        at_hi[:, pl.ds(into, size)], at_lo[:, pl.ds(into, size)] = split(ref[pl.ds(start, size), :].T)

    def project(start, size, fresh):
        def step(n, carry):
            at = pl.ds(pl.multiple_of(n * 256, 256), 256)
            if fresh:
                p_hi[:, at], p_lo[:, at] = split(w_ref[:, at])
            rows_ = pl.ds(start, size)
            hi, lo = a_hi[rows_, :], a_lo[rows_, :]
            pairs = nn_dot(hi, p_hi[:, at]) + nn_dot(hi, p_lo[:, at]) + nn_dot(lo, p_hi[:, at])
            kv_hi[rows_, at], kv_lo[rows_, at] = split(pairs)
            return carry
        lax.fori_loop(0, 4, step, 0)

    def own_pairs(start, stop):
        def step(pair, carry):
            own_part(pair, kv_hi, kv_lo, q_ref, d_ref, s_own, c_own, stats)
            return carry
        lax.fori_loop(start, stop, step, 0)

    loads[0].wait()
    pl.semaphore_wait(barrier, len(peers))
    for j in (4, 5, 2, 3, 6, 7):
        send_core(j, act.at[pl.ds(j * rows, rows)])
    slot(0)
    for j in (4, 5, 2, 3, 6, 7):
        base[j] = swap_core(j, chunk(act, j))
        if j >= 4:
            send_y(j, base.at[j])
        elif j == 3:
            slot(1)
    slot(2)
    slot(3)
    take(act, 0, 0, count)
    loads[1].wait()
    got(0)
    slot(4)
    project(0, count, True)
    loads[2].wait()
    loads[3].wait()
    got(1)
    slot(5)
    own_pairs(0, 2)
    got(2)
    slot(6)
    own_pairs(2, 4)
    for t in range(7, SLOTS):
        got(t - 4)
        slot(t)
    got(12)
    for k in range(2):
        dest[k] = arrived(k)
        send_y(k, dest.at[k])
    got(13)
    for k in range(2, 4):
        dest[k] = arrived(k)
        send_y(k, dest.at[k])
    for k in range(2):
        base[k] = swap_y(k, dest[k])
        send_core(k, base.at[k])
    for k in range(2, 4):
        set_far(k, swap_y(k, dest[k]))
    for k in range(2):
        set_far(k, swap_core(k, base[k]))
    take(far, 0, count, half)
    project(count, half, False)
    got(14)
    for k in range(4, 6):
        set_far(k, arrived(k))
    got(15)
    for k in range(6, 8):
        set_far(k, arrived(k))
    take(far, half, count + half, half)
    project(count + half, half, False)

    last = 2 * (x % 2) + ylo
    half_cp, ax_cp, ay_cp, by_cp, bx_cp, r_cp = {}, {}, {}, {}, {}, {}

    def pair_of(i):
        return (last + 1 + i) % 4

    def pair_step(i):
        far_part(pair_of(i), mask_ref, kv_hi, kv_lo, q_ref, d_ref, s_own, c_own, stats, s_far, c_far,
                 w_hi, w_lo, t_hi, t_lo, att, g_hi, g_lo)
        value = nn_dot(at_hi[...], g_hi[...]) + nn_dot(at_hi[...], g_lo[...]) + nn_dot(at_lo[...], g_hi[...])
        value = value.reshape(8, 2, 2, 2, 16, 256)
        for c in range(2):
            for kind in range(2):
                for part in range(2):
                    for yh in range(2):
                        term[i, c, kind, part, yh] = value[:, yh, c, part, :, kind * 128:(kind + 1) * 128]

    def half_copy(i):
        return remote(term.at[i, 1 - core], half_in.at[i], half_s.at[i], half_r.at[i], core_dev)

    def moves(i):
        pair = pair_of(i)
        found = []
        for kind in range(2):
            to_x = 2 * kind + pair // 2
            n = (to_x - x + 4) % 4
            slot_n = (n + 3) % 4 % 3
            found.append((n != 0, remote(total.at[i, kind, 0], ax_in.at[slot_n, pair % 2], ax_s.at[i, kind],
                                         ax_r.at[slot_n, pair % 2], device(to_x, y, z, core))))
            for yh in range(2):
                to_y = yh * 2 + pair % 2
                m = (to_y - y + 4) % 4
                slot_m = (m + 3) % 4 % 3
                found.append((m != 0, remote(total.at[i, kind, 1, yh], by_in.at[slot_m, to_x], by_s.at[i, kind, yh],
                                             by_r.at[slot_m, to_x], device(x, to_y, z, core))))
        return found

    def sum_step(i):
        half_copy(i).wait_recv()
        total[i] = term[i, core] + half_in[i]
        for condition, copy in moves(i):
            pl.when(condition)(copy.start)

    for i in range(4):
        pair_step(i)
        half_copy(i).start()
        if i > 0:
            sum_step(i - 1)
    out_copy = pltpu.make_async_copy(att, att_hbm, load_s.at[4])
    out_copy.start()
    sum_step(3)

    mine = x // 2
    for yl in range(2):
        i = (2 * (x % 2) + yl - last + 3) % 4
        value = total[i, mine, 0]
        for n in range(1, 4):
            remote(total.at[0, 0, 0], ax_in.at[n - 1, yl], ax_s.at[0, 0], ax_r.at[n - 1, yl], x_dev[n]).wait_recv()
            value = value + ax_in[n - 1, yl]
        for yh in range(2):
            ax_sum[yh * 2 + yl] = value[yh]
    for n in range(1, 4):
        ay_cp[n] = remote(ax_sum.at[(y + n) % 4], ay_in.at[n - 1], ay_s.at[n - 1], ay_r.at[n - 1], y_dev[n])
        ay_cp[n].start()
    for to_x in range(4):
        i = (2 * (to_x % 2) + ylo - last + 3) % 4
        value = total[i, to_x // 2, 1, yhi]
        for n in range(1, 4):
            remote(total.at[0, 0, 1, 0], by_in.at[n - 1, to_x], by_s.at[0, 0, 0], by_r.at[n - 1, to_x],
                   y_dev[n]).wait_recv()
            value = value + by_in[n - 1, to_x]
        by_sum[to_x] = value
    for n in range(1, 4):
        bx_cp[n] = remote(by_sum.at[(x + n) % 4], bx_in.at[n - 1], bx_s.at[n - 1], bx_r.at[n - 1], x_dev[n])
        bx_cp[n].start()
    value = ax_sum[y]
    for n in range(1, 4):
        ay_cp[n].wait_recv()
        value = value + ay_in[n - 1]
    r_out[:, 0] = value
    value = by_sum[x]
    for n in range(1, 4):
        bx_cp[n].wait_recv()
        value = value + bx_in[n - 1]
    r_out[:, 1] = value
    for n in range(1, 8):
        r_cp[n] = remote(r_out.at[(z + n) % 8], r_in.at[n - 1], r_s.at[n - 1], r_r.at[n - 1], z_dev[n])
        r_cp[n].start()
    for copies in (core_cp, y_cp, z_cp, ay_cp, bx_cp):
        for copy in copies.values():
            copy.wait_send()
    for i in range(4):
        half_copy(i).wait_send()
        for condition, copy in moves(i):
            pl.when(condition)(copy.wait_send)
    out_copy.wait()
    value = r_out[z]
    for n in range(1, 8):
        r_cp[n].wait_recv()
        value = value + r_in[n - 1]
    grad_ref[...] = value.reshape(32, 128) * (1.0 / 256.0)
    for copy in r_cp.values():
        copy.wait_send()


def run(act, queries, cotangent, w_kv, partner, mask):
    count, depth = act.shape
    width = queries.shape[1]
    rows = count // CHUNKS
    anywhere = pl.BlockSpec(memory_space=pl.ANY)
    smem = pl.BlockSpec(memory_space=pltpu.SMEM)
    vmem = pl.BlockSpec(memory_space=pltpu.VMEM)
    dma = lambda *shape: pltpu.SemaphoreType.DMA(shape)
    f32 = lambda *shape: pltpu.VMEM(shape, F32)
    b16 = lambda *shape: pltpu.VMEM(shape, BF16)
    keys, pairs = 2 * count, width // 128
    return pl.pallas_call(
        kernel,
        out_shape=(jax.ShapeDtypeStruct((count, width), F32), jax.ShapeDtypeStruct((32, 128), F32)),
        in_specs=[smem, smem] + [anywhere] * 4,
        out_specs=(anywhere, vmem),
        scratch_shapes=[
            f32(count, depth), f32(count, depth), f32(count, width), f32(count, width), f32(depth, 2 * width),
            f32(CHUNKS, rows, depth), f32(CHUNKS, rows, depth), f32(CHUNKS, rows, depth),
            f32(2, SLOTS, rows, depth), f32(2, SLOTS, rows, depth), f32(4, rows, depth),
            b16(depth, 2 * width), b16(depth, 2 * width), b16(keys, depth), b16(keys, depth),
            b16(depth, keys), b16(depth, keys), b16(keys, 2 * width), b16(keys, 2 * width),
            b16(keys, 256), b16(keys, 256), f32(pairs, count, keys), f32(pairs, count, keys), f32(pairs, 8, keys),
            f32(count, keys), f32(count, keys), b16(keys, keys), b16(keys, keys), b16(keys, keys), b16(keys, keys),
            f32(count, width),
            f32(4, 2, 2, 2, 2, 8, 16, 128), f32(4, 2, 2, 2, 8, 16, 128), f32(4, 2, 2, 2, 8, 16, 128),
            f32(3, 2, 2, 8, 16, 128), f32(4, 8, 16, 128), f32(3, 8, 16, 128),
            f32(3, 4, 8, 16, 128), f32(4, 8, 16, 128), f32(3, 8, 16, 128),
            f32(8, 2, 16, 128), f32(7, 2, 16, 128),
            dma(5), dma(CHUNKS), dma(CHUNKS), dma(CHUNKS), dma(CHUNKS), dma(2, SLOTS), dma(2, SLOTS),
            dma(4), dma(4), dma(4, 2), dma(3, 2), dma(3), dma(3), dma(4, 2, 2), dma(3, 4), dma(3), dma(3), dma(7), dma(7),
        ],
        compiler_params=pltpu.CompilerParams(collective_id=0, has_side_effects=True, vmem_limit_bytes=60 * MIB),
    )(partner, mask, act, queries, cotangent, w_kv)


def shards(activations, queries, d_out, w_kv, partner, block_mask):
    attended, gradient = run(activations[0], queries[0], d_out[0], w_kv, partner, block_mask[0, 0])
    return attended[None], gradient


def solution(mesh):
    return jax.shard_map(
        shards,
        mesh=mesh,
        in_specs=(
            P("doc", "ctx", None), P("doc", "ctx", None), P("doc", "ctx", None),
            P(), P("doc", "ctx"), P("doc", "ctx", None, None),
        ),
        out_specs=(P("doc", "ctx", None), P("ctx", "doc")),
        check_vma=False,
    )
```

```python
import functools

import jax
import jax.numpy as jnp
from jax import lax
from jax.experimental import pallas as pl
from jax.experimental.pallas import tpu as pltpu
from jax.sharding import PartitionSpec as P

MESH = pl.DeviceIdType.MESH
F32, BF16 = jnp.float32, jnp.bfloat16
MASKED = -1e30
SLOTS = 32
CHUNKS = 16
MIB = 1024 * 1024


def split(x):
    hi = x.astype(BF16)
    return hi, (x - hi.astype(F32)).astype(BF16)


def nt_dot(a, b):
    return lax.dot_general(a, b, (((1,), (1,)), ((), ())), preferred_element_type=F32)


def nn_dot(a, b):
    return lax.dot_general(a, b, (((1,), (0,)), ((), ())), preferred_element_type=F32)


def remote(src, dst, send_sem, recv_sem, device):
    return pltpu.make_async_remote_copy(
        src_ref=src, dst_ref=dst, send_sem=send_sem, recv_sem=recv_sem,
        device_id=device, device_id_type=MESH,
    )


def head_pair(x, first):
    return split(jnp.concatenate([jnp.where(first, x, 0.0), jnp.where(first, 0.0, x)], axis=0))


def cat(*parts):
    return jnp.concatenate(parts, axis=1)


def scores(kv_hi, kv_lo, rows, at, right_h, right_l):
    hi, lo = kv_hi[rows, at], kv_lo[rows, at]
    return nt_dot(cat(hi, hi, lo), cat(right_h, right_l, right_h))


def lanes_of(pair, start=0):
    return pl.ds(pl.multiple_of(start + pair * 128, 128), 128)


BLOCK = 64


def own_part(pair, kv_hi, kv_lo, q_ref, d_ref, s_own, c_own, stats):
    count, half = q_ref.shape[0], kv_hi.shape[1] // 2
    first = lax.broadcasted_iota(jnp.int32, (count, 128), 1) < 64
    at, at_v = lanes_of(pair), lanes_of(pair, half)
    q_h, q_l = head_pair(q_ref[:, at] * 0.125, first)
    d_h, d_l = head_pair(d_ref[:, at], first)
    own = pl.ds(0, count)
    s_own[pair] = scores(kv_hi, kv_lo, own, at, q_h, q_l)
    c_own[pair] = scores(kv_hi, kv_lo, own, at_v, d_h, d_l)
    maximum = jnp.max(s_own[pair, pl.ds(0, BLOCK), :], axis=0, keepdims=True)
    for b in range(1, count // BLOCK):
        maximum = jnp.maximum(maximum, jnp.max(s_own[pair, pl.ds(b * BLOCK, BLOCK), :], axis=0, keepdims=True))
    total, dots = 0.0, 0.0
    for b in range(count // BLOCK):
        rows = pl.ds(b * BLOCK, BLOCK)
        raised = jnp.exp(s_own[pair, rows, :] - maximum)
        s_own[pair, rows, :] = raised
        total = total + jnp.sum(raised, axis=0, keepdims=True)
        dots = dots + jnp.sum(raised * c_own[pair, rows, :], axis=0, keepdims=True)
    stats[pair, pl.ds(0, 1), :] = maximum
    stats[pair, pl.ds(1, 1), :] = total
    stats[pair, pl.ds(2, 1), :] = dots


def far_part(pair, mask_ref, kv_hi, kv_lo, q_ref, d_ref, s_own, c_own, stats, s_far, c_far,
             w_hi, w_lo, t_hi, t_lo, att, g_hi, g_lo):
    count, half = q_ref.shape[0], kv_hi.shape[1] // 2
    first = lax.broadcasted_iota(jnp.int32, (count, 128), 1) < 64
    at, at_v = lanes_of(pair), lanes_of(pair, half)
    q_h, q_l = head_pair(q_ref[:, at] * 0.125, first)
    d_h, d_l = head_pair(d_ref[:, at], first)
    far = pl.ds(count, count)
    s_far[...] = scores(kv_hi, kv_lo, far, at, q_h, q_l)
    c_far[...] = scores(kv_hi, kv_lo, far, at_v, d_h, d_l)
    lanes = lax.broadcasted_iota(jnp.int32, (1, 2 * count), 1) % count // BLOCK
    own_max = stats[pair, pl.ds(0, 1), :]
    maximum = own_max
    blocks = count // BLOCK
    for b in range(blocks):
        rows = pl.ds(b * BLOCK, BLOCK)
        seen = jnp.where(lanes == 0, mask_ref[0, b], jnp.where(lanes == 1, mask_ref[1, b], jnp.where(
            lanes == 2, mask_ref[2, b], mask_ref[3, b])))
        piece = jnp.where(seen == 1, s_far[rows, :], MASKED)
        s_far[rows, :] = piece
        maximum = jnp.maximum(maximum, jnp.max(piece, axis=0, keepdims=True))
    shrink = jnp.exp(own_max - maximum)
    total = stats[pair, pl.ds(1, 1), :] * shrink
    dots = stats[pair, pl.ds(2, 1), :] * shrink
    for b in range(blocks):
        rows = pl.ds(b * BLOCK, BLOCK)
        raised = jnp.exp(s_far[rows, :] - maximum)
        s_far[rows, :] = raised
        total = total + jnp.sum(raised, axis=0, keepdims=True)
        dots = dots + jnp.sum(raised * c_far[rows, :], axis=0, keepdims=True)
    inverse = 1.0 / total
    row_dot = dots * inverse
    own_scale = shrink * inverse
    for b in range(blocks):
        rows = pl.ds(b * BLOCK, BLOCK)
        weight = s_own[pair, rows, :] * own_scale
        w_hi[rows, :], w_lo[rows, :] = split(weight)
        t_hi[rows, :], t_lo[rows, :] = split(weight * (c_own[pair, rows, :] - row_dot))
        lower = pl.ds(count + b * BLOCK, BLOCK)
        weight = s_far[rows, :] * inverse
        w_hi[lower, :], w_lo[lower, :] = split(weight)
        t_hi[lower, :], t_lo[lower, :] = split(weight * (c_far[rows, :] - row_dot))

    def grads(left_hi, left_lo, right_h, right_l):
        both = nn_dot(left_hi[...], cat(right_h, right_l))
        return both[:, :128] + both[:, 128:] + nn_dot(left_lo[...], right_h)

    g_hi[:, :128], g_lo[:, :128] = split(grads(t_hi, t_lo, q_h, q_l))
    g_hi[:, 128:], g_lo[:, 128:] = split(grads(w_hi, w_lo, d_h, d_l))
    flip = lambda value: value.astype(F32).T.astype(BF16)
    vt_h, vt_l = flip(kv_hi[:, at_v]), flip(kv_lo[:, at_v])
    out = nn_dot(jnp.concatenate([vt_h, vt_l], axis=0), w_hi[...])
    out = out[:128] + out[128:] + nn_dot(vt_h, w_lo[...])
    att[:, at] = jnp.concatenate([out[:64, :count], out[64:, count:]], axis=0).T


def kernel(partner_ref, mask_ref, act_hbm, q_hbm, d_hbm, w_hbm, att_hbm, grad_ref,
           act, far, q_ref, d_ref, w_ref, core_in, base, y_in, z_out, z_in, dest,
           p_hi, p_lo, a_hi, a_lo, at_hi, at_lo, kv_hi, kv_lo, g_hi, g_lo, s_own, c_own, stats, s_far, c_far,
           w_hi, w_lo, t_hi, t_lo, att,
           term, half_in, total, ax_in, ax_sum, ay_in, by_in, by_sum, bx_in, r_out, r_in,
           load_s, core_s, core_r, y_s, y_r, z_s, z_r,
           half_s, half_r, ax_s, ax_r, ay_s, ay_r, by_s, by_r, bx_s, bx_r, r_s, r_r):
    ctx, doc = lax.axis_index("ctx"), lax.axis_index("doc")
    z, yhi, core = ctx // 4, (ctx // 2) % 2, ctx % 2
    x, ylo = doc // 2, doc % 2
    y = yhi * 2 + ylo

    def device(x_, y_, z_, core_):
        return {"ctx": z_ * 4 + (y_ // 2) * 2 + core_, "doc": x_ * 2 + y_ % 2}

    core_dev = device(x, y, z, 1 - core)
    x_dev = [None] + [device((x + n) % 4, y, z, core) for n in range(1, 4)]
    y_dev = [None] + [device(x, (y + n) % 4, z, core) for n in range(1, 4)]
    z_dev = [None] + [device(x, y, (z + n) % 8, core) for n in range(1, 8)]
    far_y = y_dev[2]
    ring_dev = (z_dev[1], z_dev[7])
    barrier = pltpu.get_barrier_semaphore()
    peers = [core_dev] + x_dev[1:] + y_dev[1:] + z_dev[1:]
    for peer in peers:
        pl.semaphore_signal(barrier, inc=1, device_id=peer, device_id_type=MESH)
    loads = [pltpu.make_async_copy(src, dst, load_s.at[n]) for n, (src, dst) in enumerate(
        ((act_hbm, act), (w_hbm, w_ref), (q_hbm, q_ref), (d_hbm, d_ref)))]
    for load in loads:
        load.start()

    offset = jnp.bitwise_xor(partner_ref[0, 0], ctx)
    flip_core = offset % 2 == 1
    flip_y = (offset // 2) % 2 == 1
    sz = offset // 4
    both_ = jnp.logical_and
    either = jnp.logical_or
    is4, is5 = sz == 4, sz == 5
    two = either(sz == 2, sz == 6)
    three = either(sz == 3, sz == 7)
    facing = (z, 7 - z)
    role = [jnp.where(sz >= 6, (zd + 2) % 4, zd % 4) for zd in facing]
    odd = [zd % 2 == 1 for zd in facing]
    count = act.shape[0]
    rows = count // CHUNKS
    core_cp, y_cp, z_cp, done = {}, {}, {}, set()

    def once(key, copy):
        if key not in done:
            done.add(key)
            copy.wait_recv()

    def chunk(ref, j):
        return ref[pl.ds(j * rows, rows), :]

    def send_core(j, src):
        core_cp[j] = remote(src, core_in.at[j], core_s.at[j], core_r.at[j], core_dev)
        core_cp[j].start()

    def send_y(j, src):
        y_cp[j] = remote(src, y_in.at[j], y_s.at[j], y_r.at[j], far_y)
        y_cp[j].start()

    def swap_core(j, value):
        once(("core", j), core_cp[j])
        return jnp.where(flip_core, core_in[j], value)

    def swap_y(j, value):
        once(("y", j), y_cp[j])
        return jnp.where(flip_y, y_in[j], value)

    def own(j):
        return chunk(act, j) if j < 8 else swap_y(j, base[j])

    def got(t):
        for d in range(2):
            once((d, t), z_cp[d, t])

    def slot(t):
        for d in range(2):
            if t < 4:
                value = own(t) if d == t == 0 else jnp.where(is4, own(2 * t + d), own(t))
            elif t < 8:
                value = jnp.where(is4, z_in[d, t - 4], own(t))
            elif t < 16:
                relay = either(both_(is5, jnp.logical_not(odd[d])), both_(three, role[d] == 1))
                value = jnp.where(is4, z_in[d, t - 4], jnp.where(relay, z_in[d, t - 8], own(t)))
            else:
                value = jnp.where(either(is5, three), z_in[d, t - 8], z_in[d, t - 16])
                if t >= 24:
                    value = jnp.where(both_(three, role[d] == 1), own(t - 16), value)
                value = jnp.where(is4, own(8 + 2 * (t - 16) + d) if t < 20 else z_in[d, t - 4], value)
            z_out[d, t] = value
            z_cp[d, t] = remote(z_out.at[d, t], z_in.at[d, t], z_s.at[d, t], z_r.at[d, t], ring_dev[d])
            z_cp[d, t].start()

    def arrived(k):
        value = own(k)
        for d in range(2):
            early = both_(sz == 1, odd[d])
            late = either(both_(two, role[d] >= 2),
                          either(both_(three, role[d] == 3), both_(is5, jnp.logical_not(odd[d]))))
            near = both_(three, role[d] == 2)
            if k < 8:
                early = either(early, near)
            else:
                late = either(late, near)
            value = jnp.where(early, z_in[d, k], value)
            value = jnp.where(late, z_in[d, 16 + k], value)
        return jnp.where(is4, z_in[k % 2, 12 + k // 2 if k < 8 else 24 + k // 2], value)

    def set_far(k, value):
        far[pl.ds(k * rows, rows), :] = value

    half = count // 2

    def take(ref, start, into, size):
        a_hi[pl.ds(into, size), :], a_lo[pl.ds(into, size), :] = split(ref[pl.ds(start, size), :])
        turned = ref[pl.ds(start, size), :].T.reshape(16, 2, 32, size)
        for c in range(2):
            hi, lo = split(turned[:, c].reshape(512, size))
            at_hi[c, :, pl.ds(into, size)], at_lo[c, :, pl.ds(into, size)] = hi, lo

    def project(start, size, fresh, n0, n1):
        def step(n, carry):
            at = pl.ds(pl.multiple_of(n * 256, 256), 256)
            if fresh:
                p_hi[:, at], p_lo[:, at] = split(w_ref[:, at])
            rows_ = pl.ds(start, size)
            hi, lo = a_hi[rows_, :], a_lo[rows_, :]
            pairs = nn_dot(hi, p_hi[:, at]) + nn_dot(hi, p_lo[:, at]) + nn_dot(lo, p_hi[:, at])
            kv_hi[rows_, at], kv_lo[rows_, at] = split(pairs)
            return carry
        lax.fori_loop(n0, n1, step, 0)

    def own_pair(pair):
        def step(n, carry):
            own_part(n, kv_hi, kv_lo, q_ref, d_ref, s_own, c_own, stats)
            return carry
        lax.fori_loop(pair, pair + 1, step, 0)

    def work(t):
        if t in (6, 7):
            take(act, (t - 6) * half, (t - 6) * half, half)
        if 8 <= t < 12:
            if t == 8:
                loads[1].wait()
            project(0, count, True, t - 8, t - 7)
        if t in (12, 13, 14, 15):
            if t == 12:
                loads[2].wait()
                loads[3].wait()
            own_pair(t - 12)

    def drain(t):
        if 16 <= t < 24:
            dest[t - 16] = arrived(t - 16)
            send_y(t - 16, dest.at[t - 16])
        if 20 <= t < 28:
            k = t - 20
            base[k] = swap_y(k, dest[k])
            send_core(k, base.at[k])
        if 22 <= t < 30:
            k = t - 22
            set_far(k, swap_core(k, base[k]))

    loads[0].wait()
    pl.semaphore_wait(barrier, len(peers))
    for j in range(8, CHUNKS):
        send_core(j, act.at[pl.ds(j * rows, rows)])
    slot(0)
    slot(1)
    for j in range(8, CHUNKS):
        base[j] = swap_core(j, chunk(act, j))
        send_y(j, base.at[j])
    slot(2)
    slot(3)
    for t in range(4, SLOTS):
        got(t - 4)
        slot(t)
        drain(t - 4)
        work(t)
    got(28)
    drain(28)
    for k in range(8, 10):
        set_far(k, arrived(k))
    got(29)
    drain(29)
    for k in range(10, 12):
        set_far(k, arrived(k))
    take(far, 0, count, half)
    project(count, half, False, 0, 4)
    for t in (30, 31):
        got(t)
        for k in range(2 * t - 48, 2 * t - 46):
            set_far(k, arrived(k))
    take(far, half, count + half, half)
    project(count + half, half, False, 0, 4)

    last = 2 * (x % 2) + ylo
    half_cp, ax_cp, ay_cp, by_cp, bx_cp, r_cp = {}, {}, {}, {}, {}, {}

    def pair_of(i):
        return (last + 1 + i) % 4

    def attend_step(i):
        far_part(pair_of(i), mask_ref, kv_hi, kv_lo, q_ref, d_ref, s_own, c_own, stats, s_far, c_far,
                 w_hi, w_lo, t_hi, t_lo, att, g_hi, g_lo)

    def term_half(i, c, into):
        hi, lo = at_hi[c], at_lo[c]
        value = nn_dot(hi, g_hi[...]) + nn_dot(hi, g_lo[...]) + nn_dot(lo, g_hi[...])
        value = value.reshape(8, 2, 2, 16, 256)
        for kind in range(2):
            for part in range(2):
                for yh in range(2):
                    into[i, kind, part, yh] = value[:, yh, part, :, kind * 128:(kind + 1) * 128]

    def half_copy(i):
        return remote(term.at[i], half_in.at[i], half_s.at[i], half_r.at[i], core_dev)

    def moves(i):
        pair = pair_of(i)
        found = []
        for kind in range(2):
            to_x = 2 * kind + pair // 2
            n = (to_x - x + 4) % 4
            slot_n = (n + 3) % 4 % 3
            found.append((n != 0, remote(total.at[i, kind, 0], ax_in.at[slot_n, pair % 2], ax_s.at[i, kind],
                                         ax_r.at[slot_n, pair % 2], device(to_x, y, z, core))))
            for yh in range(2):
                to_y = yh * 2 + pair % 2
                m = (to_y - y + 4) % 4
                slot_m = (m + 3) % 4 % 3
                found.append((m != 0, remote(total.at[i, kind, 1, yh], by_in.at[slot_m, to_x], by_s.at[i, kind, yh],
                                             by_r.at[slot_m, to_x], device(x, to_y, z, core))))
        return found

    def sum_step(i):
        half_copy(i).wait_recv()
        total[i] = total[i] + half_in[i]
        for condition, copy in moves(i):
            pl.when(condition)(copy.start)

    for i in range(4):
        attend_step(i)
        term_half(i, 1 - core, term)
        half_copy(i).start()
        if i > 0:
            sum_step(i - 1)
        term_half(i, core, total)
    out_copy = pltpu.make_async_copy(att, att_hbm, load_s.at[4])
    out_copy.start()
    sum_step(3)

    def second_x(yl):
        value = total[(2 * (x % 2) + yl - last + 3) % 4, x // 2, 0]
        for n in range(1, 4):
            remote(total.at[0, 0, 0], ax_in.at[n - 1, yl], ax_s.at[0, 0], ax_r.at[n - 1, yl], x_dev[n]).wait_recv()
            value = value + ax_in[n - 1, yl]
        for yh in range(2):
            ax_sum[yh * 2 + yl] = value[yh]

    def second_y(to_x):
        value = total[(2 * (to_x % 2) + ylo - last + 3) % 4, to_x // 2, 1, yhi]
        for n in range(1, 4):
            remote(total.at[0, 0, 1, 0], by_in.at[n - 1, to_x], by_s.at[0, 0, 0], by_r.at[n - 1, to_x],
                   y_dev[n]).wait_recv()
            value = value + by_in[n - 1, to_x]
        by_sum[to_x] = value

    for n in range(1, 4):
        ay_cp[n] = remote(ax_sum.at[(y + n) % 4], ay_in.at[n - 1], ay_s.at[n - 1], ay_r.at[n - 1], y_dev[n])
        bx_cp[n] = remote(by_sum.at[(x + n) % 4], bx_in.at[n - 1], bx_s.at[n - 1], bx_r.at[n - 1], x_dev[n])
    second_x(1 - ylo)
    ay_cp[1].start()
    ay_cp[3].start()
    for n in (1, 3):
        second_y((x + n) % 4)
        bx_cp[n].start()
    second_x(ylo)
    ay_cp[2].start()
    second_y((x + 2) % 4)
    bx_cp[2].start()
    second_y(x)
    value = ax_sum[y]
    for n in range(1, 4):
        ay_cp[n].wait_recv()
        value = value + ay_in[n - 1]
    r_out[:, 0] = value
    value = by_sum[x]
    for n in range(1, 4):
        bx_cp[n].wait_recv()
        value = value + bx_in[n - 1]
    r_out[:, 1] = value
    for n in range(1, 8):
        r_cp[n] = remote(r_out.at[(z + n) % 8], r_in.at[n - 1], r_s.at[n - 1], r_r.at[n - 1], z_dev[n])
        r_cp[n].start()
    for copies in (core_cp, y_cp, z_cp, ay_cp, bx_cp):
        for copy in copies.values():
            copy.wait_send()
    for i in range(4):
        half_copy(i).wait_send()
        for condition, copy in moves(i):
            pl.when(condition)(copy.wait_send)
    out_copy.wait()
    value = r_out[z]
    for n in range(1, 8):
        r_cp[n].wait_recv()
        value = value + r_in[n - 1]
    grad_ref[...] = value.reshape(32, 128) * (1.0 / 256.0)
    for copy in r_cp.values():
        copy.wait_send()


def run(act, queries, cotangent, w_kv, partner, mask):
    count, depth = act.shape
    width = queries.shape[1]
    rows = count // CHUNKS
    anywhere = pl.BlockSpec(memory_space=pl.ANY)
    smem = pl.BlockSpec(memory_space=pltpu.SMEM)
    vmem = pl.BlockSpec(memory_space=pltpu.VMEM)
    dma = lambda *shape: pltpu.SemaphoreType.DMA(shape)
    f32 = lambda *shape: pltpu.VMEM(shape, F32)
    b16 = lambda *shape: pltpu.VMEM(shape, BF16)
    keys, pairs = 2 * count, width // 128
    return pl.pallas_call(
        kernel,
        out_shape=(jax.ShapeDtypeStruct((count, width), F32), jax.ShapeDtypeStruct((32, 128), F32)),
        in_specs=[smem, smem] + [anywhere] * 4,
        out_specs=(anywhere, vmem),
        scratch_shapes=[
            f32(count, depth), f32(count, depth), f32(count, width), f32(count, width), f32(depth, 2 * width),
            f32(CHUNKS, rows, depth), f32(CHUNKS, rows, depth), f32(CHUNKS, rows, depth),
            f32(2, SLOTS, rows, depth), f32(2, SLOTS, rows, depth), f32(CHUNKS // 2, rows, depth),
            b16(depth, 2 * width), b16(depth, 2 * width), b16(keys, depth), b16(keys, depth),
            b16(2, depth // 2, keys), b16(2, depth // 2, keys), b16(keys, 2 * width), b16(keys, 2 * width),
            b16(keys, 256), b16(keys, 256), f32(pairs, count, keys), f32(pairs, count, keys), f32(pairs, 8, keys),
            f32(count, keys), f32(count, keys), b16(keys, keys), b16(keys, keys), b16(keys, keys), b16(keys, keys),
            f32(count, width),
            f32(4, 2, 2, 2, 8, 16, 128), f32(4, 2, 2, 2, 8, 16, 128), f32(4, 2, 2, 2, 8, 16, 128),
            f32(3, 2, 2, 8, 16, 128), f32(4, 8, 16, 128), f32(3, 8, 16, 128),
            f32(3, 4, 8, 16, 128), f32(4, 8, 16, 128), f32(3, 8, 16, 128),
            f32(8, 2, 16, 128), f32(7, 2, 16, 128),
            dma(5), dma(CHUNKS), dma(CHUNKS), dma(CHUNKS), dma(CHUNKS), dma(2, SLOTS), dma(2, SLOTS),
            dma(4), dma(4), dma(4, 2), dma(3, 2), dma(3), dma(3), dma(4, 2, 2), dma(3, 4), dma(3), dma(3), dma(7), dma(7),
        ],
        compiler_params=pltpu.CompilerParams(collective_id=0, has_side_effects=True, vmem_limit_bytes=60 * MIB),
    )(partner, mask, act, queries, cotangent, w_kv)


def shards(activations, queries, d_out, w_kv, partner, block_mask):
    attended, gradient = run(activations[0], queries[0], d_out[0], w_kv, partner, block_mask[0, 0])
    return attended[None], gradient


def solution(mesh):
    return jax.shard_map(
        shards,
        mesh=mesh,
        in_specs=(
            P("doc", "ctx", None), P("doc", "ctx", None), P("doc", "ctx", None),
            P(), P("doc", "ctx"), P("doc", "ctx", None, None),
        ),
        out_specs=(P("doc", "ctx", None), P("ctx", "doc")),
        check_vma=False,
    )
```

```python
import functools

import jax
import jax.numpy as jnp
from jax import lax
from jax.experimental import pallas as pl
from jax.experimental.pallas import tpu as pltpu
from jax.sharding import PartitionSpec as P

MESH = pl.DeviceIdType.MESH
F32, BF16 = jnp.float32, jnp.bfloat16
MASKED = -1e30
SLOTS = 32
CHUNKS = 16
MIB = 1024 * 1024


def split(x):
    hi = x.astype(BF16)
    return hi, (x - hi.astype(F32)).astype(BF16)


def nt_dot(a, b):
    return lax.dot_general(a, b, (((1,), (1,)), ((), ())), preferred_element_type=F32)


def nn_dot(a, b):
    return lax.dot_general(a, b, (((1,), (0,)), ((), ())), preferred_element_type=F32)


def remote(src, dst, send_sem, recv_sem, device):
    return pltpu.make_async_remote_copy(
        src_ref=src, dst_ref=dst, send_sem=send_sem, recv_sem=recv_sem,
        device_id=device, device_id_type=MESH,
    )


def head_pair(x, first):
    return split(jnp.concatenate([jnp.where(first, x, 0.0), jnp.where(first, 0.0, x)], axis=0))


def cat(*parts):
    return jnp.concatenate(parts, axis=1)


def scores(kv_hi, kv_lo, rows, at, right_h, right_l):
    hi, lo = kv_hi[rows, at], kv_lo[rows, at]
    return nt_dot(cat(hi, hi, lo), cat(right_h, right_l, right_h))


def lanes_of(pair, start=0):
    return pl.ds(pl.multiple_of(start + pair * 128, 128), 128)


BLOCK = 64


def weigh(kv_hi, kv_lo, rows, at_v, w_hi, w_lo):
    flip = lambda value: value.astype(F32).T.astype(BF16)
    vt_h, vt_l = flip(kv_hi[rows, at_v]), flip(kv_lo[rows, at_v])
    out = nn_dot(jnp.concatenate([vt_h, vt_l], axis=0), w_hi[rows, :])
    return out[:128] + out[128:] + nn_dot(vt_h, w_lo[rows, :])


def far_scores(pair, start, size, kv_hi, kv_lo, q_ref, d_ref, s_far, c_far):
    count, half = q_ref.shape[0], kv_hi.shape[1] // 2
    first = lax.broadcasted_iota(jnp.int32, (count, 128), 1) < 64
    at, at_v = lanes_of(pair), lanes_of(pair, half)
    rows, into = pl.ds(count + start, size), pl.ds(start, size)
    s_far[pair, into, :] = scores(kv_hi, kv_lo, rows, at, *head_pair(q_ref[:, at] * 0.125, first))
    c_far[pair, into, :] = scores(kv_hi, kv_lo, rows, at_v, *head_pair(d_ref[:, at], first))


def own_part(pair, kv_hi, kv_lo, q_ref, d_ref, s_own, c_own, stats, o_own, w_hi, w_lo):
    count, half = q_ref.shape[0], kv_hi.shape[1] // 2
    first = lax.broadcasted_iota(jnp.int32, (count, 128), 1) < 64
    at, at_v = lanes_of(pair), lanes_of(pair, half)
    q_h, q_l = head_pair(q_ref[:, at] * 0.125, first)
    d_h, d_l = head_pair(d_ref[:, at], first)
    own = pl.ds(0, count)
    s_own[pair] = scores(kv_hi, kv_lo, own, at, q_h, q_l)
    c_own[pair] = scores(kv_hi, kv_lo, own, at_v, d_h, d_l)
    maximum = jnp.max(s_own[pair, pl.ds(0, BLOCK), :], axis=0, keepdims=True)
    for b in range(1, count // BLOCK):
        maximum = jnp.maximum(maximum, jnp.max(s_own[pair, pl.ds(b * BLOCK, BLOCK), :], axis=0, keepdims=True))
    total, dots = 0.0, 0.0
    for b in range(count // BLOCK):
        rows = pl.ds(b * BLOCK, BLOCK)
        raised = jnp.exp(s_own[pair, rows, :] - maximum)
        s_own[pair, rows, :] = raised
        w_hi[rows, :], w_lo[rows, :] = split(raised)
        total = total + jnp.sum(raised, axis=0, keepdims=True)
        dots = dots + jnp.sum(raised * c_own[pair, rows, :], axis=0, keepdims=True)
    stats[pair, pl.ds(0, 1), :] = maximum
    stats[pair, pl.ds(1, 1), :] = total
    stats[pair, pl.ds(2, 1), :] = dots
    o_own[pair] = weigh(kv_hi, kv_lo, own, at_v, w_hi, w_lo)


def far_part(pair, mask_ref, kv_hi, kv_lo, q_ref, d_ref, s_own, c_own, stats, s_far, c_far, o_own,
             w_hi, w_lo, t_hi, t_lo, att, g_hi, g_lo):
    count, half = q_ref.shape[0], kv_hi.shape[1] // 2
    first = lax.broadcasted_iota(jnp.int32, (count, 128), 1) < 64
    at, at_v = lanes_of(pair), lanes_of(pair, half)
    q_h, q_l = head_pair(q_ref[:, at] * 0.125, first)
    d_h, d_l = head_pair(d_ref[:, at], first)
    far = pl.ds(count, count)
    late, into = pl.ds(count + count // 2, count // 2), pl.ds(count // 2, count // 2)
    s_far[pair, into, :] = scores(kv_hi, kv_lo, late, at, q_h, q_l)
    c_far[pair, into, :] = scores(kv_hi, kv_lo, late, at_v, d_h, d_l)
    lanes = lax.broadcasted_iota(jnp.int32, (1, 2 * count), 1) % count // BLOCK
    own_max = stats[pair, pl.ds(0, 1), :]
    maximum = own_max
    blocks = count // BLOCK
    for b in range(blocks):
        rows = pl.ds(b * BLOCK, BLOCK)
        seen = jnp.where(lanes == 0, mask_ref[0, b], jnp.where(lanes == 1, mask_ref[1, b], jnp.where(
            lanes == 2, mask_ref[2, b], mask_ref[3, b])))
        piece = jnp.where(seen == 1, s_far[pair, rows, :], MASKED)
        s_far[pair, rows, :] = piece
        maximum = jnp.maximum(maximum, jnp.max(piece, axis=0, keepdims=True))
    shrink = jnp.exp(own_max - maximum)
    total = stats[pair, pl.ds(1, 1), :] * shrink
    dots = stats[pair, pl.ds(2, 1), :] * shrink
    for b in range(blocks):
        rows = pl.ds(b * BLOCK, BLOCK)
        raised = jnp.exp(s_far[pair, rows, :] - maximum)
        s_far[pair, rows, :] = raised
        total = total + jnp.sum(raised, axis=0, keepdims=True)
        dots = dots + jnp.sum(raised * c_far[pair, rows, :], axis=0, keepdims=True)
    inverse = 1.0 / total
    row_dot = dots * inverse
    own_scale = shrink * inverse
    for b in range(blocks):
        rows = pl.ds(b * BLOCK, BLOCK)
        weight = s_own[pair, rows, :] * own_scale
        w_hi[rows, :], w_lo[rows, :] = split(weight)
        t_hi[rows, :], t_lo[rows, :] = split(weight * (c_own[pair, rows, :] - row_dot))
        lower = pl.ds(count + b * BLOCK, BLOCK)
        weight = s_far[pair, rows, :] * inverse
        w_hi[lower, :], w_lo[lower, :] = split(weight)
        t_hi[lower, :], t_lo[lower, :] = split(weight * (c_far[pair, rows, :] - row_dot))

    def grads(left_hi, left_lo, right_h, right_l):
        both = nn_dot(left_hi[...], cat(right_h, right_l))
        return both[:, :128] + both[:, 128:] + nn_dot(left_lo[...], right_h)

    g_hi[:, :128], g_lo[:, :128] = split(grads(t_hi, t_lo, q_h, q_l))
    g_hi[:, 128:], g_lo[:, 128:] = split(grads(w_hi, w_lo, d_h, d_l))
    out = o_own[pair] * own_scale + weigh(kv_hi, kv_lo, far, at_v, w_hi, w_lo)
    att[:, at] = jnp.concatenate([out[:64, :count], out[64:, count:]], axis=0).T


def kernel(partner_ref, mask_ref, act_hbm, q_hbm, d_hbm, w_hbm, att_hbm, grad_ref,
           act, far, q_ref, d_ref, w_ref, core_in, base, y_in, z_out, z_in, dest,
           p_hi, p_lo, a_hi, a_lo, at_hi, at_lo, kv_hi, kv_lo, g_hi, g_lo, s_own, c_own, stats, s_far, c_far, o_own,
           w_hi, w_lo, t_hi, t_lo, att,
           term, half_in, total, ax_in, ax_sum, ay_in, by_in, by_sum, bx_in, r_out, r_in,
           load_s, core_s, core_r, y_s, y_r, z_s, z_r,
           half_s, half_r, ax_s, ax_r, ay_s, ay_r, by_s, by_r, bx_s, bx_r, r_s, r_r):
    ctx, doc = lax.axis_index("ctx"), lax.axis_index("doc")
    z, yhi, core = ctx // 4, (ctx // 2) % 2, ctx % 2
    x, ylo = doc // 2, doc % 2
    y = yhi * 2 + ylo

    def device(x_, y_, z_, core_):
        return {"ctx": z_ * 4 + (y_ // 2) * 2 + core_, "doc": x_ * 2 + y_ % 2}

    core_dev = device(x, y, z, 1 - core)
    x_dev = [None] + [device((x + n) % 4, y, z, core) for n in range(1, 4)]
    y_dev = [None] + [device(x, (y + n) % 4, z, core) for n in range(1, 4)]
    z_dev = [None] + [device(x, y, (z + n) % 8, core) for n in range(1, 8)]
    far_y = y_dev[2]
    ring_dev = (z_dev[1], z_dev[7])
    barrier = pltpu.get_barrier_semaphore()
    peers = [core_dev] + x_dev[1:] + y_dev[1:] + z_dev[1:]
    for peer in peers:
        pl.semaphore_signal(barrier, inc=1, device_id=peer, device_id_type=MESH)
    loads = [pltpu.make_async_copy(src, dst, load_s.at[n]) for n, (src, dst) in enumerate(
        ((act_hbm, act), (w_hbm, w_ref), (q_hbm, q_ref), (d_hbm, d_ref)))]
    for load in loads:
        load.start()

    offset = jnp.bitwise_xor(partner_ref[0, 0], ctx)
    flip_core = offset % 2 == 1
    flip_y = (offset // 2) % 2 == 1
    sz = offset // 4
    both_ = jnp.logical_and
    either = jnp.logical_or
    is4, is5 = sz == 4, sz == 5
    two = either(sz == 2, sz == 6)
    three = either(sz == 3, sz == 7)
    facing = (z, 7 - z)
    role = [jnp.where(sz >= 6, (zd + 2) % 4, zd % 4) for zd in facing]
    odd = [zd % 2 == 1 for zd in facing]
    count = act.shape[0]
    rows = count // CHUNKS
    core_cp, y_cp, z_cp, done = {}, {}, {}, set()

    def once(key, copy):
        if key not in done:
            done.add(key)
            copy.wait_recv()

    def chunk(ref, j):
        return ref[pl.ds(j * rows, rows), :]

    def send_core(j, src):
        core_cp[j] = remote(src, core_in.at[j], core_s.at[j], core_r.at[j], core_dev)
        core_cp[j].start()

    def send_y(j, src):
        y_cp[j] = remote(src, y_in.at[j], y_s.at[j], y_r.at[j], far_y)
        y_cp[j].start()

    def swap_core(j, value):
        once(("core", j), core_cp[j])
        return jnp.where(flip_core, core_in[j], value)

    def swap_y(j, value):
        once(("y", j), y_cp[j])
        return jnp.where(flip_y, y_in[j], value)

    def own(j):
        return chunk(act, j) if j < 8 else swap_y(j, base[j])

    def got(t):
        for d in range(2):
            once((d, t), z_cp[d, t])

    def slot(t):
        for d in range(2):
            if t < 4:
                value = own(t) if d == t == 0 else jnp.where(is4, own(2 * t + d), own(t))
            elif t < 8:
                value = jnp.where(is4, z_in[d, t - 4], own(t))
            elif t < 16:
                relay = either(both_(is5, jnp.logical_not(odd[d])), both_(three, role[d] == 1))
                value = jnp.where(is4, z_in[d, t - 4], jnp.where(relay, z_in[d, t - 8], own(t)))
            else:
                value = jnp.where(either(is5, three), z_in[d, t - 8], z_in[d, t - 16])
                if t >= 24:
                    value = jnp.where(both_(three, role[d] == 1), own(t - 16), value)
                value = jnp.where(is4, own(8 + 2 * (t - 16) + d) if t < 20 else z_in[d, t - 4], value)
            z_out[d, t] = value
            z_cp[d, t] = remote(z_out.at[d, t], z_in.at[d, t], z_s.at[d, t], z_r.at[d, t], ring_dev[d])
            z_cp[d, t].start()

    def arrived(k):
        value = own(k)
        for d in range(2):
            early = both_(sz == 1, odd[d])
            late = either(both_(two, role[d] >= 2),
                          either(both_(three, role[d] == 3), both_(is5, jnp.logical_not(odd[d]))))
            near = both_(three, role[d] == 2)
            if k < 8:
                early = either(early, near)
            else:
                late = either(late, near)
            value = jnp.where(early, z_in[d, k], value)
            value = jnp.where(late, z_in[d, 16 + k], value)
        return jnp.where(is4, z_in[k % 2, 12 + k // 2 if k < 8 else 24 + k // 2], value)

    def set_far(k, value):
        far[pl.ds(k * rows, rows), :] = value

    half = count // 2

    def take(ref, start, into, size):
        a_hi[pl.ds(into, size), :], a_lo[pl.ds(into, size), :] = split(ref[pl.ds(start, size), :])
        turned = ref[pl.ds(start, size), :].T.reshape(16, 2, 32, size)
        for c in range(2):
            hi, lo = split(turned[:, c].reshape(512, size))
            at_hi[c, :, pl.ds(into, size)], at_lo[c, :, pl.ds(into, size)] = hi, lo

    def project(start, size, fresh, n0, n1):
        def step(n, carry):
            at = pl.ds(pl.multiple_of(n * 256, 256), 256)
            if fresh:
                p_hi[:, at], p_lo[:, at] = split(w_ref[:, at])
            rows_ = pl.ds(start, size)
            hi, lo = a_hi[rows_, :], a_lo[rows_, :]
            both = nn_dot(jnp.concatenate([hi, lo], axis=0), p_hi[:, at])
            pairs = both[:size] + both[size:] + nn_dot(hi, p_lo[:, at])
            kv_hi[rows_, at], kv_lo[rows_, at] = split(pairs)
            return carry
        lax.fori_loop(n0, n1, step, 0)

    def own_pair(pair):
        def step(n, carry):
            own_part(n, kv_hi, kv_lo, q_ref, d_ref, s_own, c_own, stats, o_own, w_hi, w_lo)
            return carry
        lax.fori_loop(pair, pair + 1, step, 0)

    def work(t):
        if t in (6, 7):
            take(act, (t - 6) * half, (t - 6) * half, half)
        if 8 <= t < 12:
            if t == 8:
                loads[1].wait()
            project(0, count, True, t - 8, t - 7)
        if t in (12, 13, 14, 15):
            if t == 12:
                loads[2].wait()
                loads[3].wait()
            own_pair(t - 12)

    def drain(t):
        if 16 <= t < 24:
            dest[t - 16] = arrived(t - 16)
            send_y(t - 16, dest.at[t - 16])
        if 19 <= t < 27:
            k = t - 19
            base[k] = swap_y(k, dest[k])
            send_core(k, base.at[k])
        if 21 <= t < 29:
            k = t - 21
            set_far(k, swap_core(k, base[k]))

    loads[0].wait()
    pl.semaphore_wait(barrier, len(peers))
    for j in range(8, CHUNKS):
        send_core(j, act.at[pl.ds(j * rows, rows)])
    slot(0)
    slot(1)
    for j in range(8, CHUNKS):
        base[j] = swap_core(j, chunk(act, j))
        send_y(j, base.at[j])
    slot(2)
    slot(3)
    for t in range(4, SLOTS):
        got(t - 4)
        slot(t)
        drain(t - 4)
        work(t)
    got(28)
    drain(28)
    take(far, 0, count, half)
    project(count, half, False, 0, 4)

    def early_scores(pair, carry):
        far_scores(pair, 0, half, kv_hi, kv_lo, q_ref, d_ref, s_far, c_far)
        return carry

    lax.fori_loop(0, 4, early_scores, 0)
    for t in range(28, 32):
        got(t)
        for k in range(2 * t - 48, 2 * t - 46):
            set_far(k, arrived(k))
    take(far, half, count + half, half)
    project(count + half, half, False, 0, 4)

    last = 2 * (x % 2) + ylo
    half_cp, ax_cp, ay_cp, by_cp, bx_cp, r_cp = {}, {}, {}, {}, {}, {}

    def pair_of(i):
        return (last + 1 + i) % 4

    def attend_step(i):
        far_part(pair_of(i), mask_ref, kv_hi, kv_lo, q_ref, d_ref, s_own, c_own, stats, s_far, c_far, o_own,
                 w_hi, w_lo, t_hi, t_lo, att, g_hi, g_lo)

    def term_half(i, c, into):
        hi, lo = at_hi[c], at_lo[c]
        value = nn_dot(hi, g_hi[...]) + nn_dot(hi, g_lo[...]) + nn_dot(lo, g_hi[...])
        value = value.reshape(8, 2, 2, 16, 256)
        for kind in range(2):
            for part in range(2):
                for yh in range(2):
                    into[i, kind, part, yh] = value[:, yh, part, :, kind * 128:(kind + 1) * 128]

    def half_copy(i):
        return remote(term.at[i], half_in.at[i], half_s.at[i], half_r.at[i], core_dev)

    def moves(i):
        pair = pair_of(i)
        found = []
        for kind in range(2):
            to_x = 2 * kind + pair // 2
            n = (to_x - x + 4) % 4
            slot_n = (n + 3) % 4 % 3
            found.append((n != 0, remote(total.at[i, kind, 0], ax_in.at[slot_n, pair % 2], ax_s.at[i, kind],
                                         ax_r.at[slot_n, pair % 2], device(to_x, y, z, core))))
            for yh in range(2):
                to_y = yh * 2 + pair % 2
                m = (to_y - y + 4) % 4
                slot_m = (m + 3) % 4 % 3
                found.append((m != 0, remote(total.at[i, kind, 1, yh], by_in.at[slot_m, to_x], by_s.at[i, kind, yh],
                                             by_r.at[slot_m, to_x], device(x, to_y, z, core))))
        return found

    def sum_step(i):
        half_copy(i).wait_recv()
        total[i] = total[i] + half_in[i]
        for condition, copy in moves(i):
            pl.when(condition)(copy.start)

    for i in range(4):
        attend_step(i)
        term_half(i, 1 - core, term)
        half_copy(i).start()
        if i > 0:
            sum_step(i - 1)
        term_half(i, core, total)
    out_copy = pltpu.make_async_copy(att, att_hbm, load_s.at[4])
    out_copy.start()
    sum_step(3)

    def second_x(yl):
        value = total[(2 * (x % 2) + yl - last + 3) % 4, x // 2, 0]
        for n in range(1, 4):
            remote(total.at[0, 0, 0], ax_in.at[n - 1, yl], ax_s.at[0, 0], ax_r.at[n - 1, yl], x_dev[n]).wait_recv()
            value = value + ax_in[n - 1, yl]
        for yh in range(2):
            ax_sum[yh * 2 + yl] = value[yh]

    def second_y(to_x):
        value = total[(2 * (to_x % 2) + ylo - last + 3) % 4, to_x // 2, 1, yhi]
        for n in range(1, 4):
            remote(total.at[0, 0, 1, 0], by_in.at[n - 1, to_x], by_s.at[0, 0, 0], by_r.at[n - 1, to_x],
                   y_dev[n]).wait_recv()
            value = value + by_in[n - 1, to_x]
        by_sum[to_x] = value

    for n in range(1, 4):
        ay_cp[n] = remote(ax_sum.at[(y + n) % 4], ay_in.at[n - 1], ay_s.at[n - 1], ay_r.at[n - 1], y_dev[n])
        bx_cp[n] = remote(by_sum.at[(x + n) % 4], bx_in.at[n - 1], bx_s.at[n - 1], bx_r.at[n - 1], x_dev[n])
    second_x(1 - ylo)
    ay_cp[1].start()
    ay_cp[3].start()
    for n in (1, 3):
        second_y((x + n) % 4)
        bx_cp[n].start()
    second_x(ylo)
    ay_cp[2].start()
    second_y((x + 2) % 4)
    bx_cp[2].start()
    second_y(x)
    value = ax_sum[y]
    for n in range(1, 4):
        ay_cp[n].wait_recv()
        value = value + ay_in[n - 1]
    r_out[:, 0] = value
    value = by_sum[x]
    for n in range(1, 4):
        bx_cp[n].wait_recv()
        value = value + bx_in[n - 1]
    r_out[:, 1] = value
    for n in range(1, 8):
        r_cp[n] = remote(r_out.at[(z + n) % 8], r_in.at[n - 1], r_s.at[n - 1], r_r.at[n - 1], z_dev[n])
        r_cp[n].start()
    for copies in (core_cp, y_cp, z_cp, ay_cp, bx_cp):
        for copy in copies.values():
            copy.wait_send()
    for i in range(4):
        half_copy(i).wait_send()
        for condition, copy in moves(i):
            pl.when(condition)(copy.wait_send)
    out_copy.wait()
    value = r_out[z]
    for n in range(1, 8):
        r_cp[n].wait_recv()
        value = value + r_in[n - 1]
    grad_ref[...] = value.reshape(32, 128) * (1.0 / 256.0)
    for copy in r_cp.values():
        copy.wait_send()


def run(act, queries, cotangent, w_kv, partner, mask):
    count, depth = act.shape
    width = queries.shape[1]
    rows = count // CHUNKS
    anywhere = pl.BlockSpec(memory_space=pl.ANY)
    smem = pl.BlockSpec(memory_space=pltpu.SMEM)
    vmem = pl.BlockSpec(memory_space=pltpu.VMEM)
    dma = lambda *shape: pltpu.SemaphoreType.DMA(shape)
    f32 = lambda *shape: pltpu.VMEM(shape, F32)
    b16 = lambda *shape: pltpu.VMEM(shape, BF16)
    keys, pairs = 2 * count, width // 128
    return pl.pallas_call(
        kernel,
        out_shape=(jax.ShapeDtypeStruct((count, width), F32), jax.ShapeDtypeStruct((32, 128), F32)),
        in_specs=[smem, smem] + [anywhere] * 4,
        out_specs=(anywhere, vmem),
        scratch_shapes=[
            f32(count, depth), f32(count, depth), f32(count, width), f32(count, width), f32(depth, 2 * width),
            f32(CHUNKS, rows, depth), f32(CHUNKS, rows, depth), f32(CHUNKS, rows, depth),
            f32(2, SLOTS, rows, depth), f32(2, SLOTS, rows, depth), f32(CHUNKS // 2, rows, depth),
            b16(depth, 2 * width), b16(depth, 2 * width), b16(keys, depth), b16(keys, depth),
            b16(2, depth // 2, keys), b16(2, depth // 2, keys), b16(keys, 2 * width), b16(keys, 2 * width),
            b16(keys, 256), b16(keys, 256), f32(pairs, count, keys), f32(pairs, count, keys), f32(pairs, 8, keys),
            f32(pairs, count, keys), f32(pairs, count, keys), f32(pairs, 128, keys), b16(keys, keys), b16(keys, keys), b16(keys, keys), b16(keys, keys),
            f32(count, width),
            f32(4, 2, 2, 2, 8, 16, 128), f32(4, 2, 2, 2, 8, 16, 128), f32(4, 2, 2, 2, 8, 16, 128),
            f32(3, 2, 2, 8, 16, 128), f32(4, 8, 16, 128), f32(3, 8, 16, 128),
            f32(3, 4, 8, 16, 128), f32(4, 8, 16, 128), f32(3, 8, 16, 128),
            f32(8, 2, 16, 128), f32(7, 2, 16, 128),
            dma(5), dma(CHUNKS), dma(CHUNKS), dma(CHUNKS), dma(CHUNKS), dma(2, SLOTS), dma(2, SLOTS),
            dma(4), dma(4), dma(4, 2), dma(3, 2), dma(3), dma(3), dma(4, 2, 2), dma(3, 4), dma(3), dma(3), dma(7), dma(7),
        ],
        compiler_params=pltpu.CompilerParams(collective_id=0, has_side_effects=True, vmem_limit_bytes=60 * MIB),
    )(partner, mask, act, queries, cotangent, w_kv)


def shards(activations, queries, d_out, w_kv, partner, block_mask):
    attended, gradient = run(activations[0], queries[0], d_out[0], w_kv, partner, block_mask[0, 0])
    return attended[None], gradient


def solution(mesh):
    return jax.shard_map(
        shards,
        mesh=mesh,
        in_specs=(
            P("doc", "ctx", None), P("doc", "ctx", None), P("doc", "ctx", None),
            P(), P("doc", "ctx"), P("doc", "ctx", None, None),
        ),
        out_specs=(P("doc", "ctx", None), P("ctx", "doc")),
        check_vma=False,
    )
```

```python
import functools

import jax
import jax.numpy as jnp
from jax import lax
from jax.experimental import pallas as pl
from jax.experimental.pallas import tpu as pltpu
from jax.sharding import PartitionSpec as P

MESH = pl.DeviceIdType.MESH
F32, BF16 = jnp.float32, jnp.bfloat16
MASKED = -1e30
SLOTS = 32
CHUNKS = 16
MIB = 1024 * 1024


def split(x):
    hi = x.astype(BF16)
    return hi, (x - hi.astype(F32)).astype(BF16)


def nt_dot(a, b):
    return lax.dot_general(a, b, (((1,), (1,)), ((), ())), preferred_element_type=F32)


def nn_dot(a, b):
    return lax.dot_general(a, b, (((1,), (0,)), ((), ())), preferred_element_type=F32)


def remote(src, dst, send_sem, recv_sem, device):
    return pltpu.make_async_remote_copy(
        src_ref=src, dst_ref=dst, send_sem=send_sem, recv_sem=recv_sem,
        device_id=device, device_id_type=MESH,
    )


def head_pair(x, first):
    return split(jnp.concatenate([jnp.where(first, x, 0.0), jnp.where(first, 0.0, x)], axis=0))


def cat(*parts):
    return jnp.concatenate(parts, axis=1)


def scores(kv_hi, kv_lo, rows, at, right_h, right_l):
    hi, lo = kv_hi[rows, at], kv_lo[rows, at]
    return nt_dot(cat(hi, hi, lo), cat(right_h, right_l, right_h))


def lanes_of(pair, start=0):
    return pl.ds(pl.multiple_of(start + pair * 128, 128), 128)


BLOCK = 64


def weigh(kv_hi, kv_lo, rows, at_v, w_hi, w_lo):
    flip = lambda value: value.astype(F32).T.astype(BF16)
    vt_h, vt_l = flip(kv_hi[rows, at_v]), flip(kv_lo[rows, at_v])
    out = nn_dot(jnp.concatenate([vt_h, vt_l], axis=0), w_hi[rows, :])
    return out[:128] + out[128:] + nn_dot(vt_h, w_lo[rows, :])


def far_scores(pair, start, size, kv_hi, kv_lo, q_ref, d_ref, s_far, c_far):
    count, half = q_ref.shape[0], kv_hi.shape[1] // 2
    first = lax.broadcasted_iota(jnp.int32, (count, 128), 1) < 64
    at, at_v = lanes_of(pair), lanes_of(pair, half)
    rows, into = pl.ds(count + start, size), pl.ds(start, size)
    s_far[pair, into, :] = scores(kv_hi, kv_lo, rows, at, *head_pair(q_ref[:, at] * 0.125, first))
    c_far[pair, into, :] = scores(kv_hi, kv_lo, rows, at_v, *head_pair(d_ref[:, at], first))


def own_part(pair, kv_hi, kv_lo, q_ref, d_ref, s_own, c_own, stats, o_own, w_hi, w_lo):
    count, half = q_ref.shape[0], kv_hi.shape[1] // 2
    first = lax.broadcasted_iota(jnp.int32, (count, 128), 1) < 64
    at, at_v = lanes_of(pair), lanes_of(pair, half)
    q_h, q_l = head_pair(q_ref[:, at] * 0.125, first)
    d_h, d_l = head_pair(d_ref[:, at], first)
    own = pl.ds(0, count)
    s_own[pair] = scores(kv_hi, kv_lo, own, at, q_h, q_l)
    c_own[pair] = scores(kv_hi, kv_lo, own, at_v, d_h, d_l)
    maximum = jnp.max(s_own[pair, pl.ds(0, BLOCK), :], axis=0, keepdims=True)
    for b in range(1, count // BLOCK):
        maximum = jnp.maximum(maximum, jnp.max(s_own[pair, pl.ds(b * BLOCK, BLOCK), :], axis=0, keepdims=True))
    total, dots = 0.0, 0.0
    for b in range(count // BLOCK):
        rows = pl.ds(b * BLOCK, BLOCK)
        raised = jnp.exp(s_own[pair, rows, :] - maximum)
        s_own[pair, rows, :] = raised
        w_hi[rows, :], w_lo[rows, :] = split(raised)
        total = total + jnp.sum(raised, axis=0, keepdims=True)
        dots = dots + jnp.sum(raised * c_own[pair, rows, :], axis=0, keepdims=True)
    stats[pair, pl.ds(0, 1), :] = maximum
    stats[pair, pl.ds(1, 1), :] = total
    stats[pair, pl.ds(2, 1), :] = dots
    o_own[pair] = weigh(kv_hi, kv_lo, own, at_v, w_hi, w_lo)


def far_part(pair, mask_ref, kv_hi, kv_lo, q_ref, d_ref, s_own, c_own, stats, s_far, c_far, o_own,
             w_hi, w_lo, t_hi, t_lo, att, g_hi, g_lo):
    count, half = q_ref.shape[0], kv_hi.shape[1] // 2
    first = lax.broadcasted_iota(jnp.int32, (count, 128), 1) < 64
    at, at_v = lanes_of(pair), lanes_of(pair, half)
    q_h, q_l = head_pair(q_ref[:, at] * 0.125, first)
    d_h, d_l = head_pair(d_ref[:, at], first)
    far = pl.ds(count, count)
    late, into = pl.ds(count + count // 2, count // 2), pl.ds(count // 2, count // 2)
    s_far[pair, into, :] = scores(kv_hi, kv_lo, late, at, q_h, q_l)
    c_far[pair, into, :] = scores(kv_hi, kv_lo, late, at_v, d_h, d_l)
    lanes = lax.broadcasted_iota(jnp.int32, (1, 2 * count), 1) % count // BLOCK
    own_max = stats[pair, pl.ds(0, 1), :]
    maximum = own_max
    blocks = count // BLOCK
    for b in range(blocks):
        rows = pl.ds(b * BLOCK, BLOCK)
        seen = jnp.where(lanes == 0, mask_ref[0, b], jnp.where(lanes == 1, mask_ref[1, b], jnp.where(
            lanes == 2, mask_ref[2, b], mask_ref[3, b])))
        piece = jnp.where(seen == 1, s_far[pair, rows, :], MASKED)
        s_far[pair, rows, :] = piece
        maximum = jnp.maximum(maximum, jnp.max(piece, axis=0, keepdims=True))
    shrink = jnp.exp(own_max - maximum)
    total = stats[pair, pl.ds(1, 1), :] * shrink
    dots = stats[pair, pl.ds(2, 1), :] * shrink
    for b in range(blocks):
        rows = pl.ds(b * BLOCK, BLOCK)
        raised = jnp.exp(s_far[pair, rows, :] - maximum)
        s_far[pair, rows, :] = raised
        total = total + jnp.sum(raised, axis=0, keepdims=True)
        dots = dots + jnp.sum(raised * c_far[pair, rows, :], axis=0, keepdims=True)
    inverse = 1.0 / total
    row_dot = dots * inverse
    own_scale = shrink * inverse
    for b in range(blocks):
        rows = pl.ds(b * BLOCK, BLOCK)
        weight = s_own[pair, rows, :] * own_scale
        w_hi[rows, :], w_lo[rows, :] = split(weight)
        t_hi[rows, :], t_lo[rows, :] = split(weight * (c_own[pair, rows, :] - row_dot))
        lower = pl.ds(count + b * BLOCK, BLOCK)
        weight = s_far[pair, rows, :] * inverse
        w_hi[lower, :], w_lo[lower, :] = split(weight)
        t_hi[lower, :], t_lo[lower, :] = split(weight * (c_far[pair, rows, :] - row_dot))

    def grads(left_hi, left_lo, right_h, right_l):
        both = nn_dot(left_hi[...], cat(right_h, right_l))
        return both[:, :128] + both[:, 128:] + nn_dot(left_lo[...], right_h)

    g_hi[:, :128], g_lo[:, :128] = split(grads(t_hi, t_lo, q_h, q_l))
    g_hi[:, 128:], g_lo[:, 128:] = split(grads(w_hi, w_lo, d_h, d_l))
    out = o_own[pair] * own_scale + weigh(kv_hi, kv_lo, far, at_v, w_hi, w_lo)
    att[:, at] = jnp.concatenate([out[:64, :count], out[64:, count:]], axis=0).T


def kernel(partner_ref, mask_ref, act_hbm, q_hbm, d_hbm, w_hbm, att_hbm, grad_ref,
           act, far, q_ref, d_ref, w_ref, core_in, base, y_in, z_out, z_in, dest,
           p_hi, p_lo, a_hi, a_lo, at_hi, at_lo, kv_hi, kv_lo, g_hi, g_lo, s_own, c_own, stats, s_far, c_far, o_own,
           w_hi, w_lo, t_hi, t_lo, att,
           term, half_in, total, ax_in, ax_sum, ay_in, by_in, by_sum, bx_in, r_out, r_in,
           load_s, core_s, core_r, y_s, y_r, z_s, z_r,
           half_s, half_r, ax_s, ax_r, ay_s, ay_r, by_s, by_r, bx_s, bx_r, r_s, r_r):
    ctx, doc = lax.axis_index("ctx"), lax.axis_index("doc")
    z, yhi, core = ctx // 4, (ctx // 2) % 2, ctx % 2
    x, ylo = doc // 2, doc % 2
    y = yhi * 2 + ylo

    def device(x_, y_, z_, core_):
        return {"ctx": z_ * 4 + (y_ // 2) * 2 + core_, "doc": x_ * 2 + y_ % 2}

    core_dev = device(x, y, z, 1 - core)
    x_dev = [None] + [device((x + n) % 4, y, z, core) for n in range(1, 4)]
    y_dev = [None] + [device(x, (y + n) % 4, z, core) for n in range(1, 4)]
    z_dev = [None] + [device(x, y, (z + n) % 8, core) for n in range(1, 8)]
    far_y = y_dev[2]
    ring_dev = (z_dev[1], z_dev[7])
    barrier = pltpu.get_barrier_semaphore()
    peers = [core_dev] + x_dev[1:] + y_dev[1:] + z_dev[1:]
    for peer in peers:
        pl.semaphore_signal(barrier, inc=1, device_id=peer, device_id_type=MESH)
    loads = [pltpu.make_async_copy(src, dst, load_s.at[n]) for n, (src, dst) in enumerate(
        ((act_hbm, act), (w_hbm, w_ref), (q_hbm, q_ref), (d_hbm, d_ref)))]
    for load in loads:
        load.start()

    offset = jnp.bitwise_xor(partner_ref[0, 0], ctx)
    flip_core = offset % 2 == 1
    flip_y = (offset // 2) % 2 == 1
    sz = offset // 4
    both_ = jnp.logical_and
    either = jnp.logical_or
    is4, is5 = sz == 4, sz == 5
    two = either(sz == 2, sz == 6)
    three = either(sz == 3, sz == 7)
    facing = (z, 7 - z)
    role = [jnp.where(sz >= 6, (zd + 2) % 4, zd % 4) for zd in facing]
    odd = [zd % 2 == 1 for zd in facing]
    count = act.shape[0]
    rows = count // CHUNKS
    core_cp, y_cp, z_cp, done = {}, {}, {}, set()

    def once(key, copy):
        if key not in done:
            done.add(key)
            copy.wait_recv()

    def chunk(ref, j):
        return ref[pl.ds(j * rows, rows), :]

    def send_core(j, src):
        core_cp[j] = remote(src, core_in.at[j], core_s.at[j], core_r.at[j], core_dev)
        core_cp[j].start()

    def send_y(j, src):
        y_cp[j] = remote(src, y_in.at[j], y_s.at[j], y_r.at[j], far_y)
        y_cp[j].start()

    def swap_core(j, value):
        once(("core", j), core_cp[j])
        return jnp.where(flip_core, core_in[j], value)

    def swap_y(j, value):
        once(("y", j), y_cp[j])
        return jnp.where(flip_y, y_in[j], value)

    def own(j):
        return chunk(act, j) if j < 8 else swap_y(j, base[j])

    def got(t):
        for d in range(2):
            once((d, t), z_cp[d, t])

    def slot(t):
        for d in range(2):
            if t < 4:
                value = own(t) if d == t == 0 else jnp.where(is4, own(2 * t + d), own(t))
            elif t < 8:
                value = jnp.where(is4, z_in[d, t - 4], own(t))
            elif t < 16:
                relay = either(both_(is5, jnp.logical_not(odd[d])), both_(three, role[d] == 1))
                value = jnp.where(is4, z_in[d, t - 4], jnp.where(relay, z_in[d, t - 8], own(t)))
            else:
                value = jnp.where(either(is5, three), z_in[d, t - 8], z_in[d, t - 16])
                if t >= 24:
                    value = jnp.where(both_(three, role[d] == 1), own(t - 16), value)
                value = jnp.where(is4, own(8 + 2 * (t - 16) + d) if t < 20 else z_in[d, t - 4], value)
            z_out[d, t] = value
            z_cp[d, t] = remote(z_out.at[d, t], z_in.at[d, t], z_s.at[d, t], z_r.at[d, t], ring_dev[d])
            z_cp[d, t].start()

    def arrived(k):
        value = own(k)
        for d in range(2):
            early = both_(sz == 1, odd[d])
            late = either(both_(two, role[d] >= 2),
                          either(both_(three, role[d] == 3), both_(is5, jnp.logical_not(odd[d]))))
            near = both_(three, role[d] == 2)
            if k < 8:
                early = either(early, near)
            else:
                late = either(late, near)
            value = jnp.where(early, z_in[d, k], value)
            value = jnp.where(late, z_in[d, 16 + k], value)
        return jnp.where(is4, z_in[k % 2, 12 + k // 2 if k < 8 else 24 + k // 2], value)

    def set_far(k, value):
        far[pl.ds(k * rows, rows), :] = value

    half = count // 2

    def take(ref, start, into, size):
        a_hi[pl.ds(into, size), :], a_lo[pl.ds(into, size), :] = split(ref[pl.ds(start, size), :])
        turned = ref[pl.ds(start, size), :].T.reshape(16, 2, 32, size)
        for c in range(2):
            hi, lo = split(turned[:, c].reshape(512, size))
            at_hi[c, :, pl.ds(into, size)], at_lo[c, :, pl.ds(into, size)] = hi, lo

    def project(start, size, fresh, n0, n1):
        def step(n, carry):
            at = pl.ds(pl.multiple_of(n * 256, 256), 256)
            if fresh:
                p_hi[:, at], p_lo[:, at] = split(w_ref[:, at])
            rows_ = pl.ds(start, size)
            hi, lo = a_hi[rows_, :], a_lo[rows_, :]
            both = nn_dot(jnp.concatenate([hi, lo], axis=0), p_hi[:, at])
            pairs = both[:size] + both[size:] + nn_dot(hi, p_lo[:, at])
            kv_hi[rows_, at], kv_lo[rows_, at] = split(pairs)
            return carry
        lax.fori_loop(n0, n1, step, 0)

    def own_pair(pair):
        def step(n, carry):
            own_part(n, kv_hi, kv_lo, q_ref, d_ref, s_own, c_own, stats, o_own, w_hi, w_lo)
            return carry
        lax.fori_loop(pair, pair + 1, step, 0)

    def work(t):
        if t in (6, 7):
            take(act, (t - 6) * half, (t - 6) * half, half)
        if 8 <= t < 12:
            if t == 8:
                loads[1].wait()
            project(0, count, True, t - 8, t - 7)
        if t in (12, 13, 14, 15):
            if t == 12:
                loads[2].wait()
                loads[3].wait()
            own_pair(t - 12)

    def drain(t):
        if 16 <= t < 24:
            dest[t - 16] = arrived(t - 16)
            send_y(t - 16, dest.at[t - 16])
        if 19 <= t < 27:
            k = t - 19
            base[k] = swap_y(k, dest[k])
            send_core(k, base.at[k])
        if 21 <= t < 29:
            k = t - 21
            set_far(k, swap_core(k, base[k]))

    loads[0].wait()
    pl.semaphore_wait(barrier, len(peers))
    for j in range(8, CHUNKS):
        send_core(j, act.at[pl.ds(j * rows, rows)])
    slot(0)
    slot(1)
    for j in range(8, CHUNKS):
        base[j] = swap_core(j, chunk(act, j))
        send_y(j, base.at[j])
    slot(2)
    slot(3)
    for t in range(4, SLOTS):
        got(t - 4)
        slot(t)
        drain(t - 4)
        work(t)
    got(28)
    drain(28)
    take(far, 0, count, half)
    project(count, half, False, 0, 4)

    def early_scores(pair, carry):
        far_scores(pair, 0, half, kv_hi, kv_lo, q_ref, d_ref, s_far, c_far)
        return carry

    lax.fori_loop(0, 4, early_scores, 0)
    for t in range(28, 32):
        got(t)
        for k in range(2 * t - 48, 2 * t - 46):
            set_far(k, arrived(k))
    take(far, half, count + half, half)
    project(count + half, half, False, 0, 4)

    last = 2 * (x % 2) + ylo
    half_cp, ax_cp, ay_cp, by_cp, bx_cp, r_cp = {}, {}, {}, {}, {}, {}

    def pair_of(i):
        return (last + 1 + i) % 4

    def attend_step(i):
        far_part(pair_of(i), mask_ref, kv_hi, kv_lo, q_ref, d_ref, s_own, c_own, stats, s_far, c_far, o_own,
                 w_hi, w_lo, t_hi, t_lo, att, g_hi, g_lo)

    def term_half(i, c, into):
        hi, lo = at_hi[c], at_lo[c]
        value = nn_dot(hi, g_hi[...]) + nn_dot(hi, g_lo[...]) + nn_dot(lo, g_hi[...])
        value = value.reshape(8, 2, 2, 16, 256)
        for kind in range(2):
            for part in range(2):
                for yh in range(2):
                    into[i, kind, part, yh] = value[:, yh, part, :, kind * 128:(kind + 1) * 128]

    def half_copy(i):
        return remote(term.at[i], half_in.at[i], half_s.at[i], half_r.at[i], core_dev)

    def moves(i):
        pair = pair_of(i)
        found = []
        for kind in range(2):
            to_x = 2 * kind + pair // 2
            n = (to_x - x + 4) % 4
            slot_n = (n + 3) % 4 % 3
            found.append((n != 0, remote(total.at[i, kind, 0], ax_in.at[slot_n, pair % 2], ax_s.at[i, kind],
                                         ax_r.at[slot_n, pair % 2], device(to_x, y, z, core))))
            for yh in range(2):
                to_y = yh * 2 + pair % 2
                m = (to_y - y + 4) % 4
                slot_m = (m + 3) % 4 % 3
                found.append((m != 0, remote(total.at[i, kind, 1, yh], by_in.at[slot_m, to_x], by_s.at[i, kind, yh],
                                             by_r.at[slot_m, to_x], device(x, to_y, z, core))))
        return found

    def sum_step(i):
        half_copy(i).wait_recv()
        total[i] = total[i] + half_in[i]
        for condition, copy in moves(i):
            pl.when(condition)(copy.start)

    for i in range(4):
        attend_step(i)
        term_half(i, 1 - core, term)
        half_copy(i).start()
        if i > 0:
            sum_step(i - 1)
        term_half(i, core, total)
    out_copy = pltpu.make_async_copy(att, att_hbm, load_s.at[4])
    out_copy.start()
    sum_step(3)

    def second_x(yl):
        value = total[(2 * (x % 2) + yl - last + 3) % 4, x // 2, 0]
        for n in range(1, 4):
            remote(total.at[0, 0, 0], ax_in.at[n - 1, yl], ax_s.at[0, 0], ax_r.at[n - 1, yl], x_dev[n]).wait_recv()
            value = value + ax_in[n - 1, yl]
        for yh in range(2):
            ax_sum[yh * 2 + yl] = value[yh]

    def second_y(to_x):
        value = total[(2 * (to_x % 2) + ylo - last + 3) % 4, to_x // 2, 1, yhi]
        for n in range(1, 4):
            remote(total.at[0, 0, 1, 0], by_in.at[n - 1, to_x], by_s.at[0, 0, 0], by_r.at[n - 1, to_x],
                   y_dev[n]).wait_recv()
            value = value + by_in[n - 1, to_x]
        by_sum[to_x] = value

    for n in range(1, 4):
        ay_cp[n] = remote(ax_sum.at[(y + n) % 4], ay_in.at[n - 1], ay_s.at[n - 1], ay_r.at[n - 1], y_dev[n])
        bx_cp[n] = remote(by_sum.at[(x + n) % 4], bx_in.at[n - 1], bx_s.at[n - 1], bx_r.at[n - 1], x_dev[n])
    second_x(1 - ylo)
    ay_cp[1].start()
    ay_cp[3].start()
    for n in (1, 3):
        second_y((x + n) % 4)
        bx_cp[n].start()
    second_x(ylo)
    ay_cp[2].start()
    second_y((x + 2) % 4)
    bx_cp[2].start()
    second_y(x)
    value = ax_sum[y]
    for n in range(1, 4):
        ay_cp[n].wait_recv()
        value = value + ay_in[n - 1]
    r_out[:, 0] = value
    value = by_sum[x]
    for n in range(1, 4):
        bx_cp[n].wait_recv()
        value = value + bx_in[n - 1]
    r_out[:, 1] = value
    for n in range(1, 8):
        r_cp[n] = remote(r_out.at[(z + n) % 8], r_in.at[n - 1], r_s.at[n - 1], r_r.at[n - 1], z_dev[n])
        r_cp[n].start()
    for copies in (core_cp, y_cp, z_cp, ay_cp, bx_cp):
        for copy in copies.values():
            copy.wait_send()
    for i in range(4):
        half_copy(i).wait_send()
        for condition, copy in moves(i):
            pl.when(condition)(copy.wait_send)
    out_copy.wait()
    value = r_out[z]
    for n in range(1, 8):
        r_cp[n].wait_recv()
        value = value + r_in[n - 1]
    grad_ref[...] = value.reshape(32, 128) * (1.0 / 256.0)
    for copy in r_cp.values():
        copy.wait_send()


def run(act, queries, cotangent, w_kv, partner, mask):
    count, depth = act.shape
    width = queries.shape[1]
    rows = count // CHUNKS
    anywhere = pl.BlockSpec(memory_space=pl.ANY)
    smem = pl.BlockSpec(memory_space=pltpu.SMEM)
    vmem = pl.BlockSpec(memory_space=pltpu.VMEM)
    dma = lambda *shape: pltpu.SemaphoreType.DMA(shape)
    f32 = lambda *shape: pltpu.VMEM(shape, F32)
    b16 = lambda *shape: pltpu.VMEM(shape, BF16)
    keys, pairs = 2 * count, width // 128
    return pl.pallas_call(
        kernel,
        out_shape=(jax.ShapeDtypeStruct((count, width), F32), jax.ShapeDtypeStruct((32, 128), F32)),
        in_specs=[smem, smem] + [anywhere] * 4,
        out_specs=(anywhere, vmem),
        scratch_shapes=[
            f32(count, depth), f32(count, depth), f32(count, width), f32(count, width), f32(depth, 2 * width),
            f32(CHUNKS, rows, depth), f32(CHUNKS, rows, depth), f32(CHUNKS, rows, depth),
            f32(2, SLOTS, rows, depth), f32(2, SLOTS, rows, depth), f32(CHUNKS // 2, rows, depth),
            b16(depth, 2 * width), b16(depth, 2 * width), b16(keys, depth), b16(keys, depth),
            b16(2, depth // 2, keys), b16(2, depth // 2, keys), b16(keys, 2 * width), b16(keys, 2 * width),
            b16(keys, 256), b16(keys, 256), f32(pairs, count, keys), f32(pairs, count, keys), f32(pairs, 8, keys),
            f32(pairs, count, keys), f32(pairs, count, keys), f32(pairs, 128, keys), b16(keys, keys), b16(keys, keys), b16(keys, keys), b16(keys, keys),
            f32(count, width),
            f32(4, 2, 2, 2, 8, 16, 128), f32(4, 2, 2, 2, 8, 16, 128), f32(4, 2, 2, 2, 8, 16, 128),
            f32(3, 2, 2, 8, 16, 128), f32(4, 8, 16, 128), f32(3, 8, 16, 128),
            f32(3, 4, 8, 16, 128), f32(4, 8, 16, 128), f32(3, 8, 16, 128),
            f32(8, 2, 16, 128), f32(7, 2, 16, 128),
            dma(5), dma(CHUNKS), dma(CHUNKS), dma(CHUNKS), dma(CHUNKS), dma(2, SLOTS), dma(2, SLOTS),
            dma(4), dma(4), dma(4, 2), dma(3, 2), dma(3), dma(3), dma(4, 2, 2), dma(3, 4), dma(3), dma(3), dma(7), dma(7),
        ],
        compiler_params=pltpu.CompilerParams(collective_id=0, has_side_effects=True, vmem_limit_bytes=60 * MIB),
    )(partner, mask, act, queries, cotangent, w_kv)


def hand_over_kernel(att_in, grad_in, att_out, grad_out, att_mid, grad_mid, in_s, out_s):
    rows = att_mid.shape[1]
    steps = [(grad_in, grad_mid, grad_out)]
    for n in range(att_mid.shape[0]):
        part = pl.ds(n * rows, rows)
        steps.append((att_in.at[part], att_mid.at[n], att_out.at[part]))
    inward = [pltpu.make_async_copy(src, mid, in_s.at[n]) for n, (src, mid, _) in enumerate(steps)]
    outward = [pltpu.make_async_copy(mid, dst, out_s.at[n]) for n, (_, mid, dst) in enumerate(steps)]
    for copy in inward:
        copy.start()
    for first, second in zip(inward, outward):
        first.wait()
        second.start()
    for copy in outward:
        copy.wait()


def hand_over(attended, gradient):
    anywhere = pl.BlockSpec(memory_space=pl.ANY)
    count, width = attended.shape
    return pl.pallas_call(
        hand_over_kernel,
        out_shape=(jax.ShapeDtypeStruct(attended.shape, F32), jax.ShapeDtypeStruct(gradient.shape, F32)),
        in_specs=[anywhere, anywhere],
        out_specs=(anywhere, anywhere),
        scratch_shapes=[
            pltpu.VMEM((4, count // 4, width), F32), pltpu.VMEM(gradient.shape, F32),
            pltpu.SemaphoreType.DMA((5,)), pltpu.SemaphoreType.DMA((5,)),
        ],
    )(attended, gradient)


def shards(activations, queries, d_out, w_kv, partner, block_mask):
    attended, gradient = run(activations[0], queries[0], d_out[0], w_kv, partner, block_mask[0, 0])
    attended, gradient = hand_over(attended, gradient)
    return attended[None], gradient


def solution(mesh):
    return jax.shard_map(
        shards,
        mesh=mesh,
        in_specs=(
            P("doc", "ctx", None), P("doc", "ctx", None), P("doc", "ctx", None),
            P(), P("doc", "ctx"), P("doc", "ctx", None, None),
        ),
        out_specs=(P("doc", "ctx", None), P("ctx", "doc")),
        check_vma=False,
    )
```
